32 devices in a mesh: row: 4 (over y, core), col: 8 (over z, x).
Axes of the slice: x: 2, y: 2, z: 4, core: 2. Of those that a mesh axis runs over, the one named last changes fastest.
Arguments:
- raw_blocks: bfloat16 [2, 4096, 4096], P(None, 'row', 'col'), may hold values from -1.25 to 1.25
- occupancy: int32 [8, 4096], P('row', 'col'), may hold values 0 or 1
- exponent: int32 [8, 8], P('row', 'col'), may hold values from -2 to 2
Outputs:
- multiples: bfloat16 [2, 2, 4096, 512], P(None, None, ('row', 'col'))
The draws below stay inside these ranges and needn't reach their ends.
All inputs are finite; a program needn't handle non-finite values. No bound on the sum of `occupancy` on one device may be relied on, other than what follows from the above.
Results may differ from the reference program's by a relative error of at most 0.02.
Values may be sent and summed in bfloat16 or wider, within the bound.
No kernel may reach another device: no remote copies, remote signals or barrier semaphores. Data moves between devices by JAX's collectives and lax.ppermute only.
A program may use at most 64 MiB of HBM per device.

```python
import jax
import jax.numpy as jnp
from jax import lax

COLS_DEV = 512
TILE = 512
TRACES = 4096
N_COL = 8


def plant(drawn, key, least, top_value):
    longest = drawn.shape.index(max(drawn.shape))
    spots = []
    for shift in (0, 1):
        where = [jax.random.randint(jax.random.fold_in(key, axis), (), 0, length) for axis, length in enumerate(drawn.shape)]
        where[longest] = (where[longest] + shift) % drawn.shape[longest]
        spots.append(tuple(where))
    return drawn.at[spots[0]].set(least).at[spots[1]].set(top_value)


def spiked(entries, stream_key, source, target, parts, factor):
    owner, partner = [(jnp.arange(entries.shape[dim]) // (entries.shape[dim] // parts)).reshape([-1 if axis == dim else 1 for axis in range(entries.ndim)]) for dim in (source, target)]
    chosen = jax.random.permutation(stream_key, parts)[partner]
    strong = (owner == chosen) | (owner == (partner + parts // 2) % parts)
    return jnp.where(strong, factor * entries, entries)


def levels(rng, shape, cuts, low, top_value):
    loudness, own = 1.0, jax.random.fold_in(rng, 6)
    for position, blocks in cuts:
        draws = jnp.exp(jax.random.uniform(jax.random.fold_in(own, position), (blocks,), jnp.float32, low / len(cuts), top_value / len(cuts)))
        loudness = loudness * jnp.repeat(draws, shape[position] // blocks).reshape([-1 if axis == position else 1 for axis in range(len(shape))])
    return loudness


def heavy_noise(key, shape, spread, reach, pieces, heavy, kind=jnp.bfloat16):
    array = spread * jax.random.normal(key, shape, jnp.float32)
    if pieces:
        array = array * levels(key, shape, pieces, -0.22, 0.18)
    return jnp.clip(spiked(array, jax.random.fold_in(key, 3), *heavy), -reach, reach).astype(kind)


def setup_inputs(seed: int = 0) -> dict:
    streams_of = jax.random.split(jax.random.key(seed), 4)
    raw_blocks = heavy_noise(streams_of[0], (2, TRACES, TRACES), (0.5 * TRACES ** -0.25), 1.25, ((1, 4), (2, 8)), (2, 1, 8, 2.0))
    occupancy = plant((jax.random.randint(streams_of[1], (TRACES // TILE, TRACES), 0, 4) < 3).astype(jnp.int32), jax.random.fold_in(streams_of[1], 1), 0, 1)
    exponent = plant(jax.random.randint(streams_of[2], (TRACES // TILE, TRACES // TILE), -2, 3), jax.random.fold_in(streams_of[2], 1), -2, 2).astype(jnp.int32)
    return {"raw_blocks": raw_blocks, "occupancy": occupancy, "exponent": exponent}


def decode(raw_blocks, occupancy, exponent):
    tile_scale = jnp.exp2(exponent.astype(jnp.float32))
    col_scale = jnp.repeat(tile_scale, TILE, axis=1)
    factor = occupancy.astype(jnp.float32) * col_scale
    shaped = raw_blocks.astype(jnp.float32).reshape(2, TRACES // TILE, TILE, TRACES) * factor[None, :, None, :]
    return shaped.reshape(2, TRACES, TRACES).astype(jnp.bfloat16)


def hdot(left_op, right_op):
    return jnp.dot(left_op, right_op, precision=lax.Precision.HIGHEST, preferred_element_type=jnp.float32)


def reference(raw_blocks, occupancy, exponent):
    decoded = decode(raw_blocks, occupancy, exponent)
    panels_out = []
    for which_panel in range(2):
        offset = which_panel * (TRACES // 2)
        panel_cols = lax.dynamic_slice_in_dim(decoded, offset, COLS_DEV, 2).astype(jnp.float32)

        def add_block(running, block_idx):
            left_op = lax.dynamic_slice_in_dim(decoded, (block_idx * COLS_DEV).astype(jnp.int32), COLS_DEV, 2).astype(jnp.float32)
            right_op = lax.dynamic_slice_in_dim(panel_cols, (block_idx * COLS_DEV).astype(jnp.int32), COLS_DEV, 1)
            real_part = hdot(left_op[0], right_op[0]) - hdot(left_op[1], right_op[1])
            imag_part = hdot(left_op[0], right_op[1]) + hdot(left_op[1], right_op[0])
            partial_value = lax.optimization_barrier(jnp.stack([real_part, imag_part]).astype(jnp.bfloat16))
            return running + partial_value.astype(jnp.float32), None

        running, _ = lax.scan(add_block, jnp.zeros((2, TRACES, COLS_DEV), jnp.float32), jnp.arange(N_COL, dtype=jnp.int32))
        panels_out.append(running.astype(jnp.bfloat16))
    return jnp.stack(panels_out)
```

```python
import functools

import jax
import jax.numpy as jnp
from jax import lax
from jax.experimental import pallas as pl
from jax.experimental.pallas import tpu as pltpu
from jax.sharding import PartitionSpec as P

WAVES = 2
VMEM_BYTES = 48 * 1024 * 1024
VMEM = pl.BlockSpec(memory_space=pltpu.VMEM)
SMEM = pl.BlockSpec(memory_space=pltpu.SMEM)
PARAMS = pltpu.CompilerParams(vmem_limit_bytes=VMEM_BYTES)


def after(value, *done):
    return lax.optimization_barrier((value,) + done)[0]


def bits_of(count):
    return list(range(count.bit_length() - 1))


def layout_kernel(x_count, raw_ref, occupancy_ref, exponent_ref, *refs):
    piece_refs, left_ref, factor_ref = refs[:-2], refs[-2], refs[-1]
    tiles = []
    for tile in range(x_count):
        row = occupancy_ref[tile : tile + 1, :].astype(jnp.float32)
        power = jnp.exp2(jnp.full(row.shape, exponent_ref[0, tile], jnp.int32).astype(jnp.float32))
        tiles.append((row * power).astype(jnp.bfloat16))
        factor_ref[tile] = tiles[tile].astype(jnp.float32)
    _, share, width = piece_refs[0].shape
    for index, out_ref in enumerate(piece_refs):
        wave, tile = divmod(index, x_count)
        columns = slice(wave * width, (wave + 1) * width)
        for part in range(2):
            out_ref[part] = raw_ref[part, tile * share : (tile + 1) * share, columns] * tiles[tile][:, columns]
    col, col_count = lax.axis_index("col"), lax.axis_size("col")
    depth = raw_ref.shape[2]
    rows = raw_ref.shape[1] // col_count
    for distance in range(col_count):
        block = col ^ distance
        factor = factor_ref[block // (col_count // x_count)].astype(jnp.bfloat16)
        start = pl.multiple_of(block * rows, rows)
        for part in range(2):
            value = raw_ref[part, pl.ds(start, rows), :] * factor
            left_ref[distance * rows : (distance + 1) * rows, part * depth : (part + 1) * depth] = value


def lay_out(raw_blocks, occupancy, exponent, x_count):
    _, length, depth = raw_blocks.shape
    piece = jax.ShapeDtypeStruct((2, length // x_count, depth // WAVES), jnp.bfloat16)
    left = jax.ShapeDtypeStruct((length, 2 * depth), jnp.bfloat16)
    count = WAVES * x_count
    out = pl.pallas_call(
        functools.partial(layout_kernel, x_count),
        out_shape=[piece] * count + [left],
        in_specs=[VMEM, VMEM, SMEM],
        out_specs=[VMEM] * (count + 1),
        scratch_shapes=[pltpu.VMEM((x_count, 1, depth), jnp.float32)],
        compiler_params=PARAMS,
    )(raw_blocks, occupancy, exponent.T)
    return out[:count], out[count]


def halves(blocks, bit):
    keep = [block for block in blocks if not block >> bit & 1]
    return [block | 1 << bit for block in keep], keep


def product_kernel(orders, mine_ref, theirs_ref, here_ref, across_ref, *refs):
    outs, slab_ref = refs[:-1], refs[-1]
    row = lax.axis_index("row")
    holds = row // 2 == row % 2
    depth, width = here_ref.shape[1:]

    def build(piece_ref):
        real, imag = piece_ref[0], piece_ref[1]
        slab_ref[:depth, :width] = real
        slab_ref[:depth, width:] = imag
        slab_ref[depth:, :width] = -imag
        slab_ref[depth:, width:] = real

    pl.when(holds)(lambda: build(here_ref))
    pl.when(jnp.logical_not(holds))(lambda: build(across_ref))
    for chain, left_ref in enumerate((mine_ref, theirs_ref)):
        send_ref, keep_ref = outs[2 * chain : 2 * chain + 2]
        blocks, _, rows, _ = send_ref.shape
        send, keep = halves(range(2 * blocks), orders[chain][0])
        value = jnp.dot(left_ref[...], slab_ref[...], preferred_element_type=jnp.float32).astype(send_ref.dtype)
        for out_ref, kept in ((send_ref, send), (keep_ref, keep)):
            for place, block in enumerate(kept):
                for part in range(2):
                    out_ref[place, part] = value[block * rows : (block + 1) * rows, part * width : (part + 1) * width]


def products(orders, mine, theirs, here, across, col_count):
    out = jax.ShapeDtypeStruct((col_count // 2, 2, mine.shape[0] // col_count, here.shape[2]), jnp.bfloat16)
    return pl.pallas_call(
        functools.partial(product_kernel, orders),
        out_shape=[out] * 4,
        in_specs=[VMEM] * 4,
        out_specs=[VMEM] * 4,
        scratch_shapes=[pltpu.VMEM((2 * here.shape[1], 2 * here.shape[2]), jnp.bfloat16)],
        compiler_params=PARAMS,
    )(mine, theirs, here, across)


def halve_kernel(orders, step, joined, *refs):
    ins, outs = refs[:4], refs[4:]
    for chain, order in enumerate(orders):
        keep_ref, other_ref = ins[2 * chain : 2 * chain + 2]
        blocks = range(1 << len(order))
        for bit in order[:step]:
            blocks = halves(blocks, bit)[1]
        blocks = list(blocks)
        for index, kept in enumerate(halves(blocks, order[step])):
            for place, block in enumerate(kept):
                at = blocks.index(block)
                total = keep_ref[at].astype(jnp.float32) + other_ref[at].astype(jnp.float32)
                if joined:
                    outs[index][chain] = total.astype(outs[index].dtype)
                else:
                    outs[2 * chain + index][place] = total.astype(outs[2 * chain + index].dtype)


def halve(orders, step, keeps, others):
    blocks, *rest = keeps[0].shape
    joined = step == len(orders[0]) - 1
    send = jax.ShapeDtypeStruct((2 if joined else blocks // 2, *rest), jnp.bfloat16)
    keep = jax.ShapeDtypeStruct(send.shape, jnp.float32)
    outs = pl.pallas_call(
        functools.partial(halve_kernel, orders, step, joined),
        out_shape=[send, keep] if joined else [send, keep] * 2,
        in_specs=[VMEM] * 4,
        out_specs=[VMEM] * (2 if joined else 4),
        compiler_params=PARAMS,
    )(keeps[0], others[0], keeps[1], others[1])
    return outs[0::2], outs[1::2]


def add_kernel(keep_ref, other_ref, out_ref):
    out_ref[...] = (keep_ref[...] + other_ref[...].astype(jnp.float32)).astype(out_ref.dtype)


def add(keep, other):
    return pl.pallas_call(
        add_kernel,
        out_shape=jax.ShapeDtypeStruct(keep.shape, jnp.bfloat16),
        in_specs=[VMEM] * 2,
        out_specs=VMEM,
        compiler_params=PARAMS,
    )(keep, other)


def solution(mesh):
    row_count, col_count = mesh.shape["row"], mesh.shape["col"]
    x_count = col_count // row_count
    y_count = row_count // 2
    half_cols = col_count // 2
    every = range(row_count * col_count)
    x_bits = bits_of(x_count)
    z_bits = [bit for bit in bits_of(col_count) if bit not in x_bits]
    orders = (x_bits + z_bits, z_bits[:1] + x_bits + z_bits[1:])
    steps = len(orders[0])
    swap_core = [(r, r ^ 1) for r in range(row_count)]

    def exchange(value, bit):
        return lax.ppermute(value, "col", [(c, c ^ (1 << bit)) for c in range(col_count)])

    def filled(pairs):
        def apart(a, b):
            (row_a, col_a), (row_b, col_b) = divmod(a, col_count), divmod(b, col_count)
            far = abs(col_a // x_count - col_b // x_count) + abs(col_a % x_count - col_b % x_count)
            return 4 * far + 4 * abs(row_a // 2 - row_b // 2) + abs(row_a - row_b)

        free = sorted(set(every) - {s for s, _ in pairs})
        for d in sorted(set(every) - {t for _, t in pairs}, key=lambda d: (d not in free, d)):
            nearest = min(free, key=lambda s: (apart(s, d), s))
            free.remove(nearest)
            pairs = pairs + [(nearest, d)]
        return pairs

    def target(s, panel, h):
        return 3 * panel * col_count + s * x_count + h

    def straight_pairs(h):
        return filled(
            [(s * col_count + p * half_cols, target(s, p, h)) for s in range(row_count) for p in range(2)]
        )

    def hop_pairs(h):
        return [(d, d ^ h if d % col_count % half_cols in (0, h) else d) for d in every]

    def spread_pairs():
        return filled(
            [
                (s * col_count + p * half_cols + h, target(s, p, h))
                for s in range(row_count)
                for p in range(2)
                for h in range(x_count)
            ]
        )

    def across_pairs():
        pairs = []
        for r in range(row_count):
            y, core = divmod(r, 2)
            pairs.append((r, r if y > 1 else r ^ 2 if y == core else r ^ 1))
        return pairs

    def to_all_y(here):
        across = lax.ppermute(here, "row", across_pairs())
        y = lax.axis_index("row") // 2
        if y_count > 2:
            slab = jnp.where(y == lax.axis_index("row") % 2, here, across)
            for bit in range(1, y_count.bit_length() - 1):
                got = lax.ppermute(slab, "row", [(r, r ^ (2 << bit)) for r in range(row_count)])
                slab = jnp.where((y >> bit) & 1 == 1, got, slab)
            return slab, slab
        return here, across

    def on_device(raw_blocks, occupancy, exponent):
        my_col = lax.axis_index("col")
        core = lax.axis_index("row") % 2
        x = my_col % x_count
        pieces, left = lay_out(raw_blocks, occupancy, exponent, x_count)

        first = None
        for h in range(x_count):
            got = lax.ppermute(pieces[h], ("row", "col"), straight_pairs(h))
            first = got if h == 0 else jnp.where(x == h, got, first)
        second = pieces[x_count]
        for h in range(1, x_count):
            got = lax.ppermute(pieces[x_count + h], ("row", "col"), hop_pairs(h))
            second = jnp.where(my_col % half_cols == h, got, second)
        first, second = lax.optimization_barrier((first, second))
        theirs = lax.ppermute(left, "row", swap_core)

        second = lax.ppermute(second, ("row", "col"), spread_pairs())
        slabs = to_all_y(first)
        outs = products(orders, left, theirs, *slabs, col_count)
        second = after(second, outs[0])
        slabs = to_all_y(second)

        sums = [None] * WAVES
        state = [None] * WAVES

        def send_step(wave, sends, keeps, step):
            if len(sends) == 1:
                state[wave] = (keeps, [exchange(sends[0], orders[0][step])])
            else:
                state[wave] = (keeps, [exchange(send, order[step]) for send, order in zip(sends, orders)])

        def next_step(wave, step):
            keeps, others = state[wave]
            if step == steps:
                sums[wave] = add(keeps[0], others[0])
            else:
                sends, keeps = halve(orders, step, keeps, others)
                send_step(wave, sends, keeps, step)

        send_step(0, outs[0::2], outs[1::2], 0)
        outs = products(orders, left, theirs, *slabs, col_count)
        send_step(1, outs[0::2], outs[1::2], 0)
        state[0] = (state[0][0], [after(other, outs[0]) for other in state[0][1]])
        for step in range(1, steps + 1):
            next_step(0, step)
            if step > 1:
                mark = sums[0] if step == steps else state[0][0][0]
                keeps, others = state[1]
                state[1] = (keeps, [after(other, mark) for other in others])
                next_step(1, step - 1)
        next_step(1, steps)

        total = jnp.concatenate(sums, axis=-1)
        back = lax.ppermute(total[1], "row", swap_core)
        return jnp.stack([jnp.where(core == 0, total[0], back), jnp.where(core == 0, back, total[0])])

    placed = (P(None, "row", "col"), P("row", "col"), P("row", "col"))
    return jax.shard_map(
        on_device,
        mesh=mesh,
        in_specs=placed,
        out_specs=P(None, None, ("row", "col"), None),
        check_vma=False,
    )
```

```python
import functools

import jax
import jax.numpy as jnp
from jax import lax
from jax.experimental import pallas as pl
from jax.experimental.pallas import tpu as pltpu
from jax.sharding import PartitionSpec as P

WAVES = 2
VMEM_BYTES = 48 * 1024 * 1024
VMEM = pl.BlockSpec(memory_space=pltpu.VMEM)
SMEM = pl.BlockSpec(memory_space=pltpu.SMEM)
PARAMS = pltpu.CompilerParams(vmem_limit_bytes=VMEM_BYTES)


def after(value, *done):
    return lax.optimization_barrier((value,) + done)[0]


def bits_of(count):
    return list(range(count.bit_length() - 1))


def layout_kernel(x_count, raw_ref, occupancy_ref, exponent_ref, *refs):
    piece_refs, left_ref, factor_ref = refs[:-2], refs[-2], refs[-1]
    tiles = []
    for tile in range(x_count):
        row = occupancy_ref[tile : tile + 1, :].astype(jnp.float32)
        power = jnp.exp2(jnp.full(row.shape, exponent_ref[0, tile], jnp.int32).astype(jnp.float32))
        tiles.append((row * power).astype(jnp.bfloat16))
        factor_ref[tile] = tiles[tile].astype(jnp.float32)
    _, share, width = piece_refs[0].shape
    for index, out_ref in enumerate(piece_refs):
        wave, tile = divmod(index, x_count)
        columns = slice(wave * width, (wave + 1) * width)
        for part in range(2):
            out_ref[part] = raw_ref[part, tile * share : (tile + 1) * share, columns] * tiles[tile][:, columns]
    col, col_count = lax.axis_index("col"), lax.axis_size("col")
    depth = raw_ref.shape[2]
    rows = raw_ref.shape[1] // col_count
    for distance in range(col_count):
        block = col ^ distance
        factor = factor_ref[block // (col_count // x_count)].astype(jnp.bfloat16)
        start = pl.multiple_of(block * rows, rows)
        for part in range(2):
            value = raw_ref[part, pl.ds(start, rows), :] * factor
            left_ref[distance * rows : (distance + 1) * rows, part * depth : (part + 1) * depth] = value


def lay_out(raw_blocks, occupancy, exponent, x_count):
    _, length, depth = raw_blocks.shape
    piece = jax.ShapeDtypeStruct((2, length // x_count, depth // WAVES), jnp.bfloat16)
    left = jax.ShapeDtypeStruct((length, 2 * depth), jnp.bfloat16)
    count = WAVES * x_count
    out = pl.pallas_call(
        functools.partial(layout_kernel, x_count),
        out_shape=[piece] * count + [left],
        in_specs=[VMEM, VMEM, SMEM],
        out_specs=[VMEM] * (count + 1),
        scratch_shapes=[pltpu.VMEM((x_count, 1, depth), jnp.float32)],
        compiler_params=PARAMS,
    )(raw_blocks, occupancy, exponent.T)
    return out[:count], out[count]


def halves(blocks, bit):
    keep = [block for block in blocks if not block >> bit & 1]
    return [block | 1 << bit for block in keep], keep


def product_kernel(orders, mine_ref, theirs_ref, here_ref, across_ref, *refs):
    outs, slab_ref = refs[:-1], refs[-1]
    row = lax.axis_index("row")
    holds = row // 2 + row % 2 == 1
    depth, width = here_ref.shape[1:]

    def build(piece_ref):
        real, imag = piece_ref[0], piece_ref[1]
        slab_ref[:depth, :width] = real
        slab_ref[:depth, width:] = imag
        slab_ref[depth:, :width] = -imag
        slab_ref[depth:, width:] = real

    pl.when(holds)(lambda: build(here_ref))
    pl.when(jnp.logical_not(holds))(lambda: build(across_ref))
    for chain, left_ref in enumerate((mine_ref, theirs_ref)):
        send_ref, keep_ref = outs[2 * chain : 2 * chain + 2]
        blocks, _, rows, _ = send_ref.shape
        send, keep = halves(range(2 * blocks), orders[chain][0])
        value = jnp.dot(left_ref[...], slab_ref[...], preferred_element_type=jnp.float32).astype(send_ref.dtype)
        for out_ref, kept in ((send_ref, send), (keep_ref, keep)):
            for place, block in enumerate(kept):
                for part in range(2):
                    out_ref[place, part] = value[block * rows : (block + 1) * rows, part * width : (part + 1) * width]


def products(orders, mine, theirs, here, across, col_count):
    out = jax.ShapeDtypeStruct((col_count // 2, 2, mine.shape[0] // col_count, here.shape[2]), jnp.bfloat16)
    return pl.pallas_call(
        functools.partial(product_kernel, orders),
        out_shape=[out] * 4,
        in_specs=[VMEM] * 4,
        out_specs=[VMEM] * 4,
        scratch_shapes=[pltpu.VMEM((2 * here.shape[1], 2 * here.shape[2]), jnp.bfloat16)],
        compiler_params=PARAMS,
    )(mine, theirs, here, across)


def halve_kernel(orders, step, joined, *refs):
    ins, outs = refs[:4], refs[4:]
    for chain, order in enumerate(orders):
        keep_ref, other_ref = ins[2 * chain : 2 * chain + 2]
        blocks = range(1 << len(order))
        for bit in order[:step]:
            blocks = halves(blocks, bit)[1]
        blocks = list(blocks)
        for index, kept in enumerate(halves(blocks, order[step])):
            for place, block in enumerate(kept):
                at = blocks.index(block)
                total = keep_ref[at].astype(jnp.float32) + other_ref[at].astype(jnp.float32)
                if joined:
                    outs[index][chain] = total.astype(outs[index].dtype)
                else:
                    outs[2 * chain + index][place] = total.astype(outs[2 * chain + index].dtype)


def halve(orders, step, keeps, others):
    blocks, *rest = keeps[0].shape
    joined = step == len(orders[0]) - 1
    send = jax.ShapeDtypeStruct((2 if joined else blocks // 2, *rest), jnp.bfloat16)
    keep = jax.ShapeDtypeStruct(send.shape, jnp.float32)
    outs = pl.pallas_call(
        functools.partial(halve_kernel, orders, step, joined),
        out_shape=[send, keep] if joined else [send, keep] * 2,
        in_specs=[VMEM] * 4,
        out_specs=[VMEM] * (2 if joined else 4),
        compiler_params=PARAMS,
    )(keeps[0], others[0], keeps[1], others[1])
    return outs[0::2], outs[1::2]


def add_kernel(keep_ref, other_ref, out_ref):
    out_ref[...] = (keep_ref[...] + other_ref[...].astype(jnp.float32)).astype(out_ref.dtype)


def add(keep, other):
    return pl.pallas_call(
        add_kernel,
        out_shape=jax.ShapeDtypeStruct(keep.shape, jnp.bfloat16),
        in_specs=[VMEM] * 2,
        out_specs=VMEM,
        compiler_params=PARAMS,
    )(keep, other)


def solution(mesh):
    row_count, col_count = mesh.shape["row"], mesh.shape["col"]
    x_count = col_count // row_count
    y_count = row_count // 2
    half_cols = col_count // 2
    every = range(row_count * col_count)
    x_bits = bits_of(x_count)
    z_bits = [bit for bit in bits_of(col_count) if bit not in x_bits]
    orders = (x_bits + z_bits, z_bits[:1] + x_bits + z_bits[1:])
    steps = len(orders[0])
    swap_core = [(r, r ^ 1) for r in range(row_count)]

    def exchange(value, bit):
        return lax.ppermute(value, "col", [(c, c ^ (1 << bit)) for c in range(col_count)])

    def filled(pairs):
        def apart(a, b):
            (row_a, col_a), (row_b, col_b) = divmod(a, col_count), divmod(b, col_count)
            far = abs(col_a // x_count - col_b // x_count) + abs(col_a % x_count - col_b % x_count)
            return 2 if a == b else 4 * far + 4 * abs(row_a // 2 - row_b // 2) + abs(row_a - row_b)

        senders = set(every) - {s for s, _ in pairs}
        receivers = set(every) - {t for _, t in pairs}
        while receivers:
            _, s, t = min((apart(s, t), s, t) for s in senders for t in receivers)
            senders.remove(s)
            receivers.remove(t)
            pairs = pairs + [(s, t)]
        return pairs

    def target(s, panel, h):
        return (2 - panel) * col_count + s * x_count + h

    def straight_pairs(h):
        return filled(
            [(s * col_count + p * half_cols, target(s, p, h)) for s in range(row_count) for p in range(2)]
        )

    def hop_pairs(h):
        return [(d, d ^ h if d % col_count % half_cols in (0, h) else d ^ col_count) for d in every]

    def spread_pairs():
        return filled(
            [
                (s * col_count + p * half_cols + h, target(s, p, h))
                for s in range(row_count)
                for p in range(2)
                for h in range(x_count)
            ]
        )

    def across_pairs():
        pairs = []
        for r in range(row_count):
            y, core = divmod(r, 2)
            pairs.append((r, r ^ 1 if y > 1 or y == core else r ^ 2))
        return pairs

    def to_all_y(here):
        across = lax.ppermute(here, "row", across_pairs())
        y = lax.axis_index("row") // 2
        if y_count > 2:
            slab = jnp.where(y + lax.axis_index("row") % 2 == 1, here, across)
            for bit in range(1, y_count.bit_length() - 1):
                got = lax.ppermute(slab, "row", [(r, r ^ (2 << bit)) for r in range(row_count)])
                slab = jnp.where((y >> bit) & 1 == 1, got, slab)
            return slab, slab
        return here, across

    def on_device(raw_blocks, occupancy, exponent):
        my_col = lax.axis_index("col")
        core = lax.axis_index("row") % 2
        x = my_col % x_count
        pieces, left = lay_out(raw_blocks, occupancy, exponent, x_count)

        straight = [lax.ppermute(pieces[h], ("row", "col"), straight_pairs(h)) for h in range(x_count)]
        second = pieces[x_count]
        for h in range(1, x_count):
            got = lax.ppermute(pieces[x_count + h], ("row", "col"), hop_pairs(h))
            second = jnp.where(my_col % half_cols == h, got, second)
        straight = [after(got, second) for got in straight]
        first = straight[0]
        for h in range(1, x_count):
            first = jnp.where(x == h, straight[h], first)
        theirs = lax.ppermute(left, "row", swap_core)

        second = lax.ppermute(second, ("row", "col"), spread_pairs())
        slabs = to_all_y(first)
        outs = products(orders, left, theirs, *slabs, col_count)
        slabs = to_all_y(second)

        sums = [None] * WAVES
        state = [None] * WAVES

        def send_step(wave, sends, keeps, step):
            if len(sends) == 1:
                state[wave] = (keeps, [exchange(sends[0], orders[0][step])])
            else:
                state[wave] = (keeps, [exchange(send, order[step]) for send, order in zip(sends, orders)])

        def next_step(wave, step):
            keeps, others = state[wave]
            if step == steps:
                sums[wave] = add(keeps[0], others[0])
            else:
                sends, keeps = halve(orders, step, keeps, others)
                send_step(wave, sends, keeps, step)

        send_step(0, outs[0::2], outs[1::2], 0)
        outs = products(orders, left, theirs, *slabs, col_count)
        send_step(1, outs[0::2], outs[1::2], 0)
        state[0] = (state[0][0], [after(other, outs[0]) for other in state[0][1]])
        for step in range(1, steps + 1):
            next_step(0, step)
            if step > 1:
                mark = sums[0] if step == steps else state[0][0][0]
                keeps, others = state[1]
                state[1] = (keeps, [after(other, mark) for other in others])
                next_step(1, step - 1)
        next_step(1, steps)

        total = jnp.concatenate(sums, axis=-1)
        back = lax.ppermute(total[1], "row", swap_core)
        return jnp.stack([jnp.where(core == 0, total[0], back), jnp.where(core == 0, back, total[0])])

    placed = (P(None, "row", "col"), P("row", "col"), P("row", "col"))
    return jax.shard_map(
        on_device,
        mesh=mesh,
        in_specs=placed,
        out_specs=P(None, None, ("row", "col"), None),
        check_vma=False,
    )
```

```python
import functools

import jax
import jax.numpy as jnp
from jax import lax
from jax.experimental import pallas as pl
from jax.experimental.pallas import tpu as pltpu
from jax.sharding import PartitionSpec as P

WAVES = 2
VMEM_BYTES = 48 * 1024 * 1024
VMEM = pl.BlockSpec(memory_space=pltpu.VMEM)
SMEM = pl.BlockSpec(memory_space=pltpu.SMEM)
PARAMS = pltpu.CompilerParams(vmem_limit_bytes=VMEM_BYTES)


def after(value, *done):
    return lax.optimization_barrier((value,) + done)[0]


def bits_of(count):
    return list(range(count.bit_length() - 1))


def layout_kernel(x_count, raw_ref, occupancy_ref, exponent_ref, *refs):
    piece_refs, left_ref, factor_ref = refs[:-2], refs[-2], refs[-1]
    tiles = []
    for tile in range(x_count):
        row = occupancy_ref[tile : tile + 1, :].astype(jnp.float32)
        power = jnp.exp2(jnp.full(row.shape, exponent_ref[0, tile], jnp.int32).astype(jnp.float32))
        tiles.append((row * power).astype(jnp.bfloat16))
        factor_ref[tile] = tiles[tile].astype(jnp.float32)
    _, share, width = piece_refs[0].shape
    for index, out_ref in enumerate(piece_refs):
        wave, tile = divmod(index, x_count)
        columns = slice(wave * width, (wave + 1) * width)
        for part in range(2):
            out_ref[part] = raw_ref[part, tile * share : (tile + 1) * share, columns] * tiles[tile][:, columns]
    col, col_count = lax.axis_index("col"), lax.axis_size("col")
    depth = raw_ref.shape[2]
    rows = raw_ref.shape[1] // col_count
    for distance in range(col_count):
        block = col ^ distance
        factor = factor_ref[block // (col_count // x_count)].astype(jnp.bfloat16)
        start = pl.multiple_of(block * rows, rows)
        for part in range(2):
            value = raw_ref[part, pl.ds(start, rows), :] * factor
            left_ref[distance * rows : (distance + 1) * rows, part * depth : (part + 1) * depth] = value


def lay_out(raw_blocks, occupancy, exponent, x_count):
    _, length, depth = raw_blocks.shape
    piece = jax.ShapeDtypeStruct((2, length // x_count, depth // WAVES), jnp.bfloat16)
    left = jax.ShapeDtypeStruct((length, 2 * depth), jnp.bfloat16)
    count = WAVES * x_count
    out = pl.pallas_call(
        functools.partial(layout_kernel, x_count),
        out_shape=[piece] * count + [left],
        in_specs=[VMEM, VMEM, SMEM],
        out_specs=[VMEM] * (count + 1),
        scratch_shapes=[pltpu.VMEM((x_count, 1, depth), jnp.float32)],
        compiler_params=PARAMS,
    )(raw_blocks, occupancy, exponent.T)
    return out[:count], out[count]


def halves(blocks, bit):
    keep = [block for block in blocks if not block >> bit & 1]
    return [block | 1 << bit for block in keep], keep


def product_kernel(orders, index, mine_ref, theirs_ref, here_ref, across_ref, *refs):
    outs, slab_ref = refs[:-1], refs[-1]
    row = lax.axis_index("row")
    holds = row // 2 + row % 2 == 1
    depth, width = here_ref.shape[1:]

    def build(piece_ref):
        real, imag = piece_ref[0], piece_ref[1]
        slab_ref[:depth, :width] = real
        slab_ref[:depth, width:] = imag
        slab_ref[depth:, :width] = -imag
        slab_ref[depth:, width:] = real

    pl.when(holds)(lambda: build(here_ref))
    pl.when(jnp.logical_not(holds))(lambda: build(across_ref))
    for order, left_ref, out_ref in zip(orders, (mine_ref, theirs_ref), outs):
        count, _, rows, _ = out_ref.shape
        blocks = halves(range(2 * count), order[0])[index]
        left = jnp.concatenate([left_ref[block * rows : (block + 1) * rows, :] for block in blocks])
        value = jnp.dot(left, slab_ref[...], preferred_element_type=jnp.float32).astype(out_ref.dtype)
        for place in range(count):
            for part in range(2):
                out_ref[place, part] = value[place * rows : (place + 1) * rows, part * width : (part + 1) * width]


def products(orders, index, mine, theirs, here, across, col_count):
    out = jax.ShapeDtypeStruct((col_count // 2, 2, mine.shape[0] // col_count, here.shape[2]), jnp.bfloat16)
    return pl.pallas_call(
        functools.partial(product_kernel, orders, index),
        out_shape=[out] * 2,
        in_specs=[VMEM] * 4,
        out_specs=[VMEM] * 2,
        scratch_shapes=[pltpu.VMEM((2 * here.shape[1], 2 * here.shape[2]), jnp.bfloat16)],
        compiler_params=PARAMS,
    )(mine, theirs, here, across)


def halve_kernel(orders, step, joined, *refs):
    ins, outs = refs[:4], refs[4:]
    for chain, order in enumerate(orders):
        keep_ref, other_ref = ins[2 * chain : 2 * chain + 2]
        blocks = range(1 << len(order))
        for bit in order[:step]:
            blocks = halves(blocks, bit)[1]
        blocks = list(blocks)
        for index, kept in enumerate(halves(blocks, order[step])):
            for place, block in enumerate(kept):
                at = blocks.index(block)
                total = keep_ref[at].astype(jnp.float32) + other_ref[at].astype(jnp.float32)
                if joined:
                    outs[index][chain] = total.astype(outs[index].dtype)
                else:
                    outs[2 * chain + index][place] = total.astype(outs[2 * chain + index].dtype)


def halve(orders, step, keeps, others):
    blocks, *rest = keeps[0].shape
    joined = step == len(orders[0]) - 1
    send = jax.ShapeDtypeStruct((2 if joined else blocks // 2, *rest), jnp.bfloat16)
    keep = jax.ShapeDtypeStruct(send.shape, jnp.float32)
    outs = pl.pallas_call(
        functools.partial(halve_kernel, orders, step, joined),
        out_shape=[send, keep] if joined else [send, keep] * 2,
        in_specs=[VMEM] * 4,
        out_specs=[VMEM] * (2 if joined else 4),
        compiler_params=PARAMS,
    )(keeps[0], others[0], keeps[1], others[1])
    return outs[0::2], outs[1::2]


def add_kernel(keep_ref, other_ref, *out_refs):
    for chain, out_ref in enumerate(out_refs):
        out_ref[...] = (keep_ref[chain] + other_ref[chain].astype(jnp.float32)).astype(out_ref.dtype)


def add(keep, other):
    return pl.pallas_call(
        add_kernel,
        out_shape=[jax.ShapeDtypeStruct(keep.shape[1:], jnp.bfloat16)] * 2,
        in_specs=[VMEM] * 2,
        out_specs=[VMEM] * 2,
        compiler_params=PARAMS,
    )(keep, other)


def place_kernel(*refs):
    out_ref = refs[-1]
    core = lax.axis_index("row") % 2
    for half, panel in enumerate((core, 1 - core)):
        begin = 0
        for ref in refs[half * WAVES : (half + 1) * WAVES]:
            width = ref.shape[-1]
            out_ref[panel, :, :, begin : begin + width] = ref[...]
            begin += width


def place(own, back, depth):
    return pl.pallas_call(
        place_kernel,
        out_shape=jax.ShapeDtypeStruct((2, *own[0].shape[:-1], depth), jnp.bfloat16),
        in_specs=[VMEM] * (2 * WAVES),
        out_specs=VMEM,
        compiler_params=PARAMS,
    )(*own, *back)


def solution(mesh):
    row_count, col_count = mesh.shape["row"], mesh.shape["col"]
    x_count = col_count // row_count
    y_count = row_count // 2
    half_cols = col_count // 2
    every = range(row_count * col_count)
    x_bits = bits_of(x_count)
    z_bits = [bit for bit in bits_of(col_count) if bit not in x_bits]
    orders = (x_bits + z_bits, z_bits[:1] + x_bits + z_bits[1:])
    steps = len(orders[0])
    swap_core = [(r, r ^ 1) for r in range(row_count)]

    def exchange(value, bit):
        return lax.ppermute(value, "col", [(c, c ^ (1 << bit)) for c in range(col_count)])

    def filled(pairs):
        def apart(a, b):
            (row_a, col_a), (row_b, col_b) = divmod(a, col_count), divmod(b, col_count)
            far = abs(col_a // x_count - col_b // x_count) + abs(col_a % x_count - col_b % x_count)
            return 2 if a == b else 4 * far + 4 * abs(row_a // 2 - row_b // 2) + abs(row_a - row_b)

        senders = set(every) - {s for s, _ in pairs}
        receivers = set(every) - {t for _, t in pairs}
        while receivers:
            _, s, t = min((apart(s, t), s, t) for s in senders for t in receivers)
            senders.remove(s)
            receivers.remove(t)
            pairs = pairs + [(s, t)]
        return pairs

    def target(s, panel, h):
        return (2 - panel) * col_count + s * x_count + h

    def straight_pairs(h):
        return filled(
            [(s * col_count + p * half_cols, target(s, p, h)) for s in range(row_count) for p in range(2)]
        )

    def hop_pairs(h):
        return [(d, d ^ h if d % col_count % half_cols in (0, h) else d ^ col_count) for d in every]

    def spread_pairs():
        return filled(
            [
                (s * col_count + p * half_cols + h, target(s, p, h))
                for s in range(row_count)
                for p in range(2)
                for h in range(x_count)
            ]
        )

    def across_pairs():
        pairs = []
        for r in range(row_count):
            y, core = divmod(r, 2)
            pairs.append((r, r ^ 1 if y > 1 or y == core else r ^ 2))
        return pairs

    def to_all_y(here):
        across = lax.ppermute(here, "row", across_pairs())
        y = lax.axis_index("row") // 2
        if y_count > 2:
            slab = jnp.where(y + lax.axis_index("row") % 2 == 1, here, across)
            for bit in range(1, y_count.bit_length() - 1):
                got = lax.ppermute(slab, "row", [(r, r ^ (2 << bit)) for r in range(row_count)])
                slab = jnp.where((y >> bit) & 1 == 1, got, slab)
            return slab, slab
        return here, across

    def exchange_step(sends, step):
        if len(sends) == 1:
            return [exchange(sends[0], orders[0][step])]
        return [exchange(send, order[step]) for send, order in zip(sends, orders)]

    def on_device(raw_blocks, occupancy, exponent):
        my_col = lax.axis_index("col")
        x = my_col % x_count
        pieces, left = lay_out(raw_blocks, occupancy, exponent, x_count)

        straight = [lax.ppermute(pieces[h], ("row", "col"), straight_pairs(h)) for h in range(x_count)]
        second = pieces[x_count]
        for h in range(1, x_count):
            got = lax.ppermute(pieces[x_count + h], ("row", "col"), hop_pairs(h))
            second = jnp.where(my_col % half_cols == h, got, second)
        straight = [after(got, second) for got in straight]
        first = straight[0]
        for h in range(1, x_count):
            first = jnp.where(x == h, straight[h], first)
        theirs = lax.ppermute(left, "row", swap_core)

        second = lax.ppermute(second, ("row", "col"), spread_pairs())
        slabs = [to_all_y(first), to_all_y(second)]

        sends = [[], []]
        sends[0] = products(orders, 0, left, theirs, *slabs[0], col_count)
        others = exchange_step(sends[0], 0)
        keeps = products(orders, 1, left, theirs, *[after(slab, sends[0][0]) for slab in slabs[0]], col_count)
        sends[1] = products(orders, 0, left, theirs, *[after(slab, keeps[0]) for slab in slabs[1]], col_count)
        later = exchange_step(sends[1], 0)
        others = [after(other, sends[1][0]) for other in others]
        sends[0], keeps = halve(orders, 1, keeps, others)
        others = exchange_step(sends[0], 1)
        stay = products(orders, 1, left, theirs, *[after(slab, sends[0][0]) for slab in slabs[1]], col_count)
        sends[0], keeps = halve(orders, 2, keeps, [after(other, stay[0]) for other in others])
        others = exchange_step(sends[0], 2)
        for step in range(1, steps):
            if step + 1 == steps - 1:
                mine, other_rows = add(keeps[0], others[0])
                own, back = [mine], [lax.ppermute(other_rows, "row", swap_core)]
                mark = mine
            elif step + 1 < steps - 1:
                sends[0], keeps = halve(orders, step + 2, keeps, others)
                others = exchange_step(sends[0], step + 2)
                mark = sends[0][0]
            if step > 1:
                later = [after(other, mark) for other in later]
            sends[1], stay = halve(orders, step, stay, later)
            later = exchange_step(sends[1], step)
        mine, other_rows = add(stay[0], later[0])
        own.append(mine)
        back.append(lax.ppermute(other_rows, "row", swap_core))
        return place(own, back, raw_blocks.shape[2])

    placed = (P(None, "row", "col"), P("row", "col"), P("row", "col"))
    return jax.shard_map(
        on_device,
        mesh=mesh,
        in_specs=placed,
        out_specs=P(None, None, ("row", "col"), None),
        check_vma=False,
    )
```

```python
import functools

import jax
import jax.numpy as jnp
from jax import lax
from jax.experimental import pallas as pl
from jax.experimental.pallas import tpu as pltpu
from jax.sharding import PartitionSpec as P

WAVES = 2
VMEM_BYTES = 48 * 1024 * 1024
VMEM = pl.BlockSpec(memory_space=pltpu.VMEM)
SMEM = pl.BlockSpec(memory_space=pltpu.SMEM)
PARAMS = pltpu.CompilerParams(vmem_limit_bytes=VMEM_BYTES)


def after(value, *done):
    return lax.optimization_barrier((value,) + done)[0]


def bits_of(count):
    return list(range(count.bit_length() - 1))


def layout_kernel(x_count, raw_ref, occupancy_ref, exponent_ref, *refs):
    piece_refs, left_ref, factor_ref = refs[:-2], refs[-2], refs[-1]
    tiles = []
    for tile in range(x_count):
        row = occupancy_ref[tile : tile + 1, :].astype(jnp.float32)
        power = jnp.exp2(jnp.full(row.shape, exponent_ref[0, tile], jnp.int32).astype(jnp.float32))
        tiles.append((row * power).astype(jnp.bfloat16))
        factor_ref[tile] = tiles[tile].astype(jnp.float32)
    _, share, width = piece_refs[0].shape
    for index, out_ref in enumerate(piece_refs):
        wave, tile = divmod(index, x_count)
        columns = slice(wave * width, (wave + 1) * width)
        for part in range(2):
            out_ref[part] = raw_ref[part, tile * share : (tile + 1) * share, columns] * tiles[tile][:, columns]
    col, col_count = lax.axis_index("col"), lax.axis_size("col")
    depth = raw_ref.shape[2]
    rows = raw_ref.shape[1] // col_count
    for distance in range(col_count):
        block = col ^ distance
        factor = factor_ref[block // (col_count // x_count)].astype(jnp.bfloat16)
        start = pl.multiple_of(block * rows, rows)
        for part in range(2):
            value = raw_ref[part, pl.ds(start, rows), :] * factor
            left_ref[distance * rows : (distance + 1) * rows, part * depth : (part + 1) * depth] = value


def lay_out(raw_blocks, occupancy, exponent, x_count):
    _, length, depth = raw_blocks.shape
    piece = jax.ShapeDtypeStruct((2, length // x_count, depth // WAVES), jnp.bfloat16)
    left = jax.ShapeDtypeStruct((length, 2 * depth), jnp.bfloat16)
    count = WAVES * x_count
    out = pl.pallas_call(
        functools.partial(layout_kernel, x_count),
        out_shape=[piece] * count + [left],
        in_specs=[VMEM, VMEM, SMEM],
        out_specs=[VMEM] * (count + 1),
        scratch_shapes=[pltpu.VMEM((x_count, 1, depth), jnp.float32)],
        compiler_params=PARAMS,
    )(raw_blocks, occupancy, exponent.T)
    return out[:count], out[count]


def halves(blocks, bit):
    keep = [block for block in blocks if not block >> bit & 1]
    return [block | 1 << bit for block in keep], keep


def product_kernel(orders, index, mine_ref, theirs_ref, here_ref, across_ref, *refs):
    outs, slab_ref = refs[:-1], refs[-1]
    row = lax.axis_index("row")
    holds = row // 2 + row % 2 == 1
    depth, width = here_ref.shape[1:]

    def build(piece_ref):
        real, imag = piece_ref[0], piece_ref[1]
        slab_ref[:depth, :width] = real
        slab_ref[:depth, width:] = imag
        slab_ref[depth:, :width] = -imag
        slab_ref[depth:, width:] = real

    pl.when(holds)(lambda: build(here_ref))
    pl.when(jnp.logical_not(holds))(lambda: build(across_ref))
    for order, left_ref, out_ref in zip(orders, (mine_ref, theirs_ref), outs):
        count, _, rows, _ = out_ref.shape
        blocks = halves(range(2 * count), order[0])[index]
        left = jnp.concatenate([left_ref[block * rows : (block + 1) * rows, :] for block in blocks])
        value = jnp.dot(left, slab_ref[...], preferred_element_type=jnp.float32).astype(out_ref.dtype)
        for place in range(count):
            for part in range(2):
                out_ref[place, part] = value[place * rows : (place + 1) * rows, part * width : (part + 1) * width]


def products(orders, index, mine, theirs, here, across, col_count):
    out = jax.ShapeDtypeStruct((col_count // 2, 2, mine.shape[0] // col_count, here.shape[2]), jnp.bfloat16)
    return pl.pallas_call(
        functools.partial(product_kernel, orders, index),
        out_shape=[out] * 2,
        in_specs=[VMEM] * 4,
        out_specs=[VMEM] * 2,
        scratch_shapes=[pltpu.VMEM((2 * here.shape[1], 2 * here.shape[2]), jnp.bfloat16)],
        compiler_params=PARAMS,
    )(mine, theirs, here, across)


def halve_kernel(orders, step, joined, *refs):
    ins, outs = refs[:4], refs[4:]
    for chain, order in enumerate(orders):
        keep_ref, other_ref = ins[2 * chain : 2 * chain + 2]
        blocks = range(1 << len(order))
        for bit in order[:step]:
            blocks = halves(blocks, bit)[1]
        blocks = list(blocks)
        for index, kept in enumerate(halves(blocks, order[step])):
            for place, block in enumerate(kept):
                at = blocks.index(block)
                total = keep_ref[at].astype(jnp.float32) + other_ref[at].astype(jnp.float32)
                if joined:
                    outs[index][chain] = total.astype(outs[index].dtype)
                else:
                    outs[2 * chain + index][place] = total.astype(outs[2 * chain + index].dtype)


def halve(orders, step, keeps, others):
    blocks, *rest = keeps[0].shape
    joined = step == len(orders[0]) - 1 and orders[0][step] == orders[1][step]
    send = jax.ShapeDtypeStruct((2 if joined else blocks // 2, *rest), jnp.bfloat16)
    keep = jax.ShapeDtypeStruct(send.shape, jnp.float32)
    outs = pl.pallas_call(
        functools.partial(halve_kernel, orders, step, joined),
        out_shape=[send, keep] if joined else [send, keep] * 2,
        in_specs=[VMEM] * 4,
        out_specs=[VMEM] * (2 if joined else 4),
        compiler_params=PARAMS,
    )(keeps[0], others[0], keeps[1], others[1])
    return outs[0::2], outs[1::2]


def add_kernel(joined, *refs):
    ins, outs = refs[:-2], refs[-2:]
    for chain, out_ref in enumerate(outs):
        keep_ref, other_ref = ins if joined else ins[2 * chain : 2 * chain + 2]
        at = chain if joined else 0
        out_ref[...] = (keep_ref[at] + other_ref[at].astype(jnp.float32)).astype(out_ref.dtype)


def add(keeps, others):
    return pl.pallas_call(
        functools.partial(add_kernel, len(keeps) == 1),
        out_shape=[jax.ShapeDtypeStruct(keeps[0].shape[1:], jnp.bfloat16)] * 2,
        in_specs=[VMEM] * (2 * len(keeps)),
        out_specs=[VMEM] * 2,
        compiler_params=PARAMS,
    )(*[value for pair in zip(keeps, others) for value in pair])


def place_kernel(*refs):
    out_ref = refs[-1]
    core = lax.axis_index("row") % 2
    for half, panel in enumerate((core, 1 - core)):
        begin = 0
        for ref in refs[half * WAVES : (half + 1) * WAVES]:
            width = ref.shape[-1]
            out_ref[panel, :, :, begin : begin + width] = ref[...]
            begin += width


def place(own, back, depth):
    return pl.pallas_call(
        place_kernel,
        out_shape=jax.ShapeDtypeStruct((2, *own[0].shape[:-1], depth), jnp.bfloat16),
        in_specs=[VMEM] * (2 * WAVES),
        out_specs=VMEM,
        compiler_params=PARAMS,
    )(*own, *back)


def solution(mesh):
    row_count, col_count = mesh.shape["row"], mesh.shape["col"]
    x_count = col_count // row_count
    y_count = row_count // 2
    half_cols = col_count // 2
    every = range(row_count * col_count)
    x_bits = bits_of(x_count)
    z_bits = [bit for bit in bits_of(col_count) if bit not in x_bits]
    orders = (
        (x_bits + z_bits, z_bits[:1] + x_bits + z_bits[1:]),
        (x_bits + z_bits, z_bits[-1:] + x_bits + z_bits[:-1]),
    )
    steps = len(x_bits + z_bits)
    swap_core = [(r, r ^ 1) for r in range(row_count)]

    def exchange(value, bit):
        return lax.ppermute(value, "col", [(c, c ^ (1 << bit)) for c in range(col_count)])

    def filled(pairs):
        def apart(a, b):
            (row_a, col_a), (row_b, col_b) = divmod(a, col_count), divmod(b, col_count)
            far = abs(col_a // x_count - col_b // x_count) + abs(col_a % x_count - col_b % x_count)
            return 2 if a == b else 4 * far + 4 * abs(row_a // 2 - row_b // 2) + abs(row_a - row_b)

        senders = set(every) - {s for s, _ in pairs}
        receivers = set(every) - {t for _, t in pairs}
        while receivers:
            _, s, t = min((apart(s, t), s, t) for s in senders for t in receivers)
            senders.remove(s)
            receivers.remove(t)
            pairs = pairs + [(s, t)]
        return pairs

    def target(s, panel, h):
        return (2 - panel) * col_count + s * x_count + h

    def straight_pairs(h):
        return filled(
            [(s * col_count + p * half_cols, target(s, p, h)) for s in range(row_count) for p in range(2)]
        )

    def hop_pairs(h):
        return [(d, d ^ h if d % col_count % half_cols in (0, h) else d ^ col_count) for d in every]

    def spread_pairs():
        return filled(
            [
                (s * col_count + p * half_cols + h, target(s, p, h))
                for s in range(row_count)
                for p in range(2)
                for h in range(x_count)
            ]
        )

    def across_pairs():
        pairs = []
        for r in range(row_count):
            y, core = divmod(r, 2)
            pairs.append((r, r ^ 1 if y > 1 or y == core else r ^ 2))
        return pairs

    def to_all_y(here):
        across = lax.ppermute(here, "row", across_pairs())
        y = lax.axis_index("row") // 2
        if y_count > 2:
            slab = jnp.where(y + lax.axis_index("row") % 2 == 1, here, across)
            for bit in range(1, y_count.bit_length() - 1):
                got = lax.ppermute(slab, "row", [(r, r ^ (2 << bit)) for r in range(row_count)])
                slab = jnp.where((y >> bit) & 1 == 1, got, slab)
            return slab, slab
        return here, across

    def exchange_step(wave, sends, step):
        return [exchange(send, order[step]) for send, order in zip(sends, orders[wave])]

    def on_device(raw_blocks, occupancy, exponent):
        my_col = lax.axis_index("col")
        x = my_col % x_count
        pieces, left = lay_out(raw_blocks, occupancy, exponent, x_count)

        straight = [lax.ppermute(pieces[h], ("row", "col"), straight_pairs(h)) for h in range(x_count)]
        second = pieces[x_count]
        for h in range(1, x_count):
            got = lax.ppermute(pieces[x_count + h], ("row", "col"), hop_pairs(h))
            second = jnp.where(my_col % half_cols == h, got, second)
        straight = [after(got, second) for got in straight]
        first = straight[0]
        for h in range(1, x_count):
            first = jnp.where(x == h, straight[h], first)
        theirs = lax.ppermute(left, "row", swap_core)

        second = lax.ppermute(second, ("row", "col"), spread_pairs())
        slabs = [to_all_y(first), to_all_y(second)]

        sends = [[], []]
        sends[0] = products(orders[0], 0, left, theirs, *slabs[0], col_count)
        others = exchange_step(0, sends[0], 0)
        keeps = products(orders[0], 1, left, theirs, *[after(slab, sends[0][0]) for slab in slabs[0]], col_count)
        sends[1] = products(orders[1], 0, left, theirs, *[after(slab, keeps[0]) for slab in slabs[1]], col_count)
        later = exchange_step(1, sends[1], 0)
        others = [after(other, sends[1][0]) for other in others]
        sends[0], keeps = halve(orders[0], 1, keeps, others)
        others = exchange_step(0, sends[0], 1)
        stay = products(orders[1], 1, left, theirs, *[after(slab, sends[0][0]) for slab in slabs[1]], col_count)
        sends[0], keeps = halve(orders[0], 2, keeps, [after(other, stay[0]) for other in others])
        others = exchange_step(0, sends[0], 2)
        for step in range(1, steps):
            if step + 1 == steps - 1:
                mine, other_rows = add(keeps, others)
                own, back = [mine], [lax.ppermute(other_rows, "row", swap_core)]
                mark = mine
            elif step + 1 < steps - 1:
                sends[0], keeps = halve(orders[0], step + 2, keeps, others)
                others = exchange_step(0, sends[0], step + 2)
                mark = sends[0][0]
            if step > 1:
                later = [after(other, mark) for other in later]
            sends[1], stay = halve(orders[1], step, stay, later)
            later = exchange_step(1, sends[1], step)
        mine, other_rows = add(stay, later)
        own.append(mine)
        back.append(lax.ppermute(other_rows, "row", swap_core))
        return place(own, back, raw_blocks.shape[2])

    placed = (P(None, "row", "col"), P("row", "col"), P("row", "col"))
    return jax.shard_map(
        on_device,
        mesh=mesh,
        in_specs=placed,
        out_specs=P(None, None, ("row", "col"), None),
        check_vma=False,
    )
```

```python
import functools

import jax
import jax.numpy as jnp
from jax import lax
from jax.experimental import pallas as pl
from jax.experimental.pallas import tpu as pltpu
from jax.sharding import PartitionSpec as P

WAVES = 2
VMEM_BYTES = 48 * 1024 * 1024
VMEM = pl.BlockSpec(memory_space=pltpu.VMEM)
PARAMS = pltpu.CompilerParams(vmem_limit_bytes=VMEM_BYTES)


def after(value, *done):
    return lax.optimization_barrier((value,) + done)[0]


def bits_of(count):
    return list(range(count.bit_length() - 1))


def layout_kernel(x_count, raw_hbm, occupancy_hbm, exponent_hbm, *refs):
    count = WAVES * x_count
    piece_refs, left_ref = refs[:count], refs[count]
    raw_ref, occupancy_ref, exponent_ref, factor_ref, small, large = refs[count + 1 :]
    _, share, width = piece_refs[0].shape
    occupancy_copy = pltpu.make_async_copy(occupancy_hbm, occupancy_ref, small.at[0])
    exponent_copy = pltpu.make_async_copy(exponent_hbm, exponent_ref, small.at[1])
    copies = []
    for tile in range(x_count):
        rows = pl.ds(tile * share, share)
        copies.append(pltpu.make_async_copy(raw_hbm.at[:, rows], raw_ref.at[:, rows], large.at[tile]))
    occupancy_copy.start()
    exponent_copy.start()
    for copy in copies:
        copy.start()
    occupancy_copy.wait()
    exponent_copy.wait()
    for tile, copy in enumerate(copies):
        row = occupancy_ref[tile : tile + 1, :].astype(jnp.float32)
        power = jnp.exp2(jnp.broadcast_to(exponent_ref[:, tile : tile + 1], row.shape).astype(jnp.float32))
        factor = (row * power).astype(jnp.bfloat16)
        factor_ref[tile] = factor.astype(jnp.float32)
        copy.wait()
        for wave in range(WAVES):
            columns = slice(wave * width, (wave + 1) * width)
            for part in range(2):
                value = raw_ref[part, tile * share : (tile + 1) * share, columns]
                piece_refs[wave * x_count + tile][part] = value * factor[:, columns]
    col, col_count = lax.axis_index("col"), lax.axis_size("col")
    depth = raw_ref.shape[2]
    rows = raw_ref.shape[1] // col_count
    for distance in range(col_count):
        block = col ^ distance
        factor = factor_ref[block // (col_count // x_count)].astype(jnp.bfloat16)
        start = pl.multiple_of(block * rows, rows)
        for part in range(2):
            value = raw_ref[part, pl.ds(start, rows), :] * factor
            left_ref[distance * rows : (distance + 1) * rows, part * depth : (part + 1) * depth] = value


def lay_out(raw_blocks, occupancy, exponent, x_count):
    _, length, depth = raw_blocks.shape
    piece = jax.ShapeDtypeStruct((2, length // x_count, depth // WAVES), jnp.bfloat16)
    left = jax.ShapeDtypeStruct((length, 2 * depth), jnp.bfloat16)
    count = WAVES * x_count
    out = pl.pallas_call(
        functools.partial(layout_kernel, x_count),
        out_shape=[piece] * count + [left],
        in_specs=[pl.BlockSpec(memory_space=pl.ANY)] * 3,
        out_specs=[VMEM] * (count + 1),
        scratch_shapes=[
            pltpu.VMEM(raw_blocks.shape, jnp.bfloat16),
            pltpu.VMEM(occupancy.shape, jnp.int32),
            pltpu.VMEM(exponent.shape[::-1], jnp.int32),
            pltpu.VMEM((x_count, 1, depth), jnp.float32),
            pltpu.SemaphoreType.DMA((2,)),
            pltpu.SemaphoreType.DMA((x_count,)),
        ],
        compiler_params=PARAMS,
    )(raw_blocks, occupancy, exponent.T)
    return out[:count], out[count]


def pick_kernel(*refs):
    options, out_ref = refs[:-1], refs[-1]
    x = lax.axis_index("col") % len(options)
    for place, option_ref in enumerate(options):

        @pl.when(x == place)
        def _(option_ref=option_ref):
            out_ref[...] = option_ref[...]


def pick(options):
    return pl.pallas_call(
        pick_kernel,
        out_shape=jax.ShapeDtypeStruct(options[0].shape, options[0].dtype),
        in_specs=[VMEM] * len(options),
        out_specs=VMEM,
        compiler_params=PARAMS,
    )(*options)


def halves(blocks, bit):
    keep = [block for block in blocks if not block >> bit & 1]
    return [block | 1 << bit for block in keep], keep


def product_kernel(orders, index, mine_ref, theirs_ref, here_ref, across_ref, *refs):
    outs, slab_ref = refs[:-1], refs[-1]
    row = lax.axis_index("row")
    holds = row // 2 + row % 2 == 1
    depth, width = here_ref.shape[1:]

    def build(piece_ref):
        real, imag = piece_ref[0], piece_ref[1]
        slab_ref[:depth, :width] = real
        slab_ref[:depth, width:] = imag
        slab_ref[depth:, :width] = -imag
        slab_ref[depth:, width:] = real

    pl.when(holds)(lambda: build(here_ref))
    pl.when(jnp.logical_not(holds))(lambda: build(across_ref))
    for order, left_ref, out_ref in zip(orders, (mine_ref, theirs_ref), outs):
        count, _, rows, _ = out_ref.shape
        blocks = halves(range(2 * count), order[0])[index]
        left = jnp.concatenate([left_ref[block * rows : (block + 1) * rows, :] for block in blocks])
        value = jnp.dot(left, slab_ref[...], preferred_element_type=jnp.float32).astype(out_ref.dtype)
        for place in range(count):
            for part in range(2):
                out_ref[place, part] = value[place * rows : (place + 1) * rows, part * width : (part + 1) * width]


def products(orders, index, mine, theirs, here, across, col_count):
    out = jax.ShapeDtypeStruct((col_count // 2, 2, mine.shape[0] // col_count, here.shape[2]), jnp.bfloat16)
    return pl.pallas_call(
        functools.partial(product_kernel, orders, index),
        out_shape=[out] * 2,
        in_specs=[VMEM] * 4,
        out_specs=[VMEM] * 2,
        scratch_shapes=[pltpu.VMEM((2 * here.shape[1], 2 * here.shape[2]), jnp.bfloat16)],
        compiler_params=PARAMS,
    )(mine, theirs, here, across)


def halve_kernel(orders, step, joined, *refs):
    ins, outs = refs[:4], refs[4:]
    for chain, order in enumerate(orders):
        keep_ref, other_ref = ins[2 * chain : 2 * chain + 2]
        blocks = range(1 << len(order))
        for bit in order[:step]:
            blocks = halves(blocks, bit)[1]
        blocks = list(blocks)
        for index, kept in enumerate(halves(blocks, order[step])):
            for place, block in enumerate(kept):
                at = blocks.index(block)
                total = keep_ref[at].astype(jnp.float32) + other_ref[at].astype(jnp.float32)
                if joined:
                    outs[index][chain] = total.astype(outs[index].dtype)
                else:
                    outs[2 * chain + index][place] = total.astype(outs[2 * chain + index].dtype)


def halve(orders, step, keeps, others):
    blocks, *rest = keeps[0].shape
    joined = step == len(orders[0]) - 1 and orders[0][step] == orders[1][step]
    send = jax.ShapeDtypeStruct((2 if joined else blocks // 2, *rest), jnp.bfloat16)
    keep = jax.ShapeDtypeStruct(send.shape, jnp.float32)
    outs = pl.pallas_call(
        functools.partial(halve_kernel, orders, step, joined),
        out_shape=[send, keep] if joined else [send, keep] * 2,
        in_specs=[VMEM] * 4,
        out_specs=[VMEM] * (2 if joined else 4),
        compiler_params=PARAMS,
    )(keeps[0], others[0], keeps[1], others[1])
    return outs[0::2], outs[1::2]


def add_kernel(joined, *refs):
    ins, outs = refs[:-2], refs[-2:]
    for chain, out_ref in enumerate(outs):
        keep_ref, other_ref = ins if joined else ins[2 * chain : 2 * chain + 2]
        at = chain if joined else 0
        out_ref[...] = (keep_ref[at] + other_ref[at].astype(jnp.float32)).astype(out_ref.dtype)


def add(keeps, others):
    return pl.pallas_call(
        functools.partial(add_kernel, len(keeps) == 1),
        out_shape=[jax.ShapeDtypeStruct(keeps[0].shape[1:], jnp.bfloat16)] * 2,
        in_specs=[VMEM] * (2 * len(keeps)),
        out_specs=[VMEM] * 2,
        compiler_params=PARAMS,
    )(*[value for pair in zip(keeps, others) for value in pair])


def place_kernel(*refs):
    out_ref = refs[-1]
    core = lax.axis_index("row") % 2
    for half, panel in enumerate((core, 1 - core)):
        begin = 0
        for ref in refs[half * WAVES : (half + 1) * WAVES]:
            width = ref.shape[-1]
            out_ref[panel, :, :, begin : begin + width] = ref[...]
            begin += width


def place(own, back, depth):
    return pl.pallas_call(
        place_kernel,
        out_shape=jax.ShapeDtypeStruct((2, *own[0].shape[:-1], depth), jnp.bfloat16),
        in_specs=[VMEM] * (2 * WAVES),
        out_specs=VMEM,
        compiler_params=PARAMS,
    )(*own, *back)


def solution(mesh):
    row_count, col_count = mesh.shape["row"], mesh.shape["col"]
    x_count = col_count // row_count
    y_count = row_count // 2
    half_cols = col_count // 2
    every = range(row_count * col_count)
    x_bits = bits_of(x_count)
    z_bits = [bit for bit in bits_of(col_count) if bit not in x_bits]
    orders = (
        (x_bits + z_bits, z_bits[:1] + x_bits + z_bits[1:]),
        (x_bits + z_bits, z_bits[-1:] + x_bits + z_bits[:-1]),
    )
    steps = len(x_bits + z_bits)
    swap_core = [(r, r ^ 1) for r in range(row_count)]

    def exchange(value, bit):
        return lax.ppermute(value, "col", [(c, c ^ (1 << bit)) for c in range(col_count)])

    def filled(pairs):
        def apart(a, b):
            (row_a, col_a), (row_b, col_b) = divmod(a, col_count), divmod(b, col_count)
            far = abs(col_a // x_count - col_b // x_count) + abs(col_a % x_count - col_b % x_count)
            return 2 if a == b else 4 * far + 4 * abs(row_a // 2 - row_b // 2) + abs(row_a - row_b)

        senders = set(every) - {s for s, _ in pairs}
        receivers = set(every) - {t for _, t in pairs}
        while receivers:
            _, s, t = min((apart(s, t), s, t) for s in senders for t in receivers)
            senders.remove(s)
            receivers.remove(t)
            pairs = pairs + [(s, t)]
        return pairs

    def target(s, panel, h):
        return (2 - panel) * col_count + s * x_count + h

    def straight_pairs(h):
        return filled(
            [(s * col_count + p * half_cols, target(s, p, h)) for s in range(row_count) for p in range(2)]
        )

    def hop_pairs(h):
        return [(d, d ^ h if d % col_count % half_cols in (0, h) else d ^ col_count) for d in every]

    def spread_pairs():
        return filled(
            [
                (s * col_count + p * half_cols + h, target(s, p, h))
                for s in range(row_count)
                for p in range(2)
                for h in range(x_count)
            ]
        )

    def across_pairs():
        pairs = []
        for r in range(row_count):
            y, core = divmod(r, 2)
            pairs.append((r, r ^ 1 if y > 1 or y == core else r ^ 2))
        return pairs

    def to_all_y(here):
        across = lax.ppermute(here, "row", across_pairs())
        y = lax.axis_index("row") // 2
        if y_count > 2:
            slab = jnp.where(y + lax.axis_index("row") % 2 == 1, here, across)
            for bit in range(1, y_count.bit_length() - 1):
                got = lax.ppermute(slab, "row", [(r, r ^ (2 << bit)) for r in range(row_count)])
                slab = jnp.where((y >> bit) & 1 == 1, got, slab)
            return slab, slab
        return here, across

    def exchange_step(wave, sends, step):
        return [exchange(send, order[step]) for send, order in zip(sends, orders[wave])]

    def on_device(raw_blocks, occupancy, exponent):
        my_col = lax.axis_index("col")
        pieces, left = lay_out(raw_blocks, occupancy, exponent, x_count)

        straight = [lax.ppermute(pieces[h], ("row", "col"), straight_pairs(h)) for h in range(x_count)]
        second = pieces[x_count]
        for h in range(1, x_count):
            got = lax.ppermute(pieces[x_count + h], ("row", "col"), hop_pairs(h))
            second = jnp.where(my_col % half_cols == h, got, second)
        first = pick([after(got, second) for got in straight])
        theirs = lax.ppermute(left, "row", swap_core)

        second = lax.ppermute(second, ("row", "col"), spread_pairs())
        slabs = [to_all_y(first), to_all_y(second)]

        sends = [[], []]
        sends[0] = products(orders[0], 0, left, theirs, *slabs[0], col_count)
        others = exchange_step(0, sends[0], 0)
        keeps = products(orders[0], 1, left, theirs, *[after(slab, sends[0][0]) for slab in slabs[0]], col_count)
        sends[1] = products(orders[1], 0, left, theirs, *[after(slab, keeps[0]) for slab in slabs[1]], col_count)
        later = exchange_step(1, sends[1], 0)
        others = [after(other, sends[1][0]) for other in others]
        sends[0], keeps = halve(orders[0], 1, keeps, others)
        others = exchange_step(0, sends[0], 1)
        stay = products(orders[1], 1, left, theirs, *[after(slab, sends[0][0]) for slab in slabs[1]], col_count)
        sends[0], keeps = halve(orders[0], 2, keeps, [after(other, stay[0]) for other in others])
        others = exchange_step(0, sends[0], 2)
        for step in range(1, steps):
            if step + 1 == steps - 1:
                mine, other_rows = add(keeps, others)
                own, back = [mine], [lax.ppermute(other_rows, "row", swap_core)]
                mark = mine
            elif step + 1 < steps - 1:
                sends[0], keeps = halve(orders[0], step + 2, keeps, others)
                others = exchange_step(0, sends[0], step + 2)
                mark = sends[0][0]
            if step > 1:
                later = [after(other, mark) for other in later]
            sends[1], stay = halve(orders[1], step, stay, later)
            later = exchange_step(1, sends[1], step)
        mine, other_rows = add(stay, later)
        own.append(mine)
        back.append(lax.ppermute(other_rows, "row", swap_core))
        return place(own, back, raw_blocks.shape[2])

    placed = (P(None, "row", "col"), P("row", "col"), P("row", "col"))
    return jax.shard_map(
        on_device,
        mesh=mesh,
        in_specs=placed,
        out_specs=P(None, None, ("row", "col"), None),
        check_vma=False,
    )
```

```python
import functools

import jax
import jax.numpy as jnp
from jax import lax
from jax.experimental import pallas as pl
from jax.experimental.pallas import tpu as pltpu
from jax.sharding import PartitionSpec as P

WAVES = 2
VMEM_BYTES = 20 * 1024 * 1024
VMEM = pl.BlockSpec(memory_space=pltpu.VMEM)
PARAMS = pltpu.CompilerParams(vmem_limit_bytes=VMEM_BYTES)


def after(value, *done):
    return lax.optimization_barrier((value,) + done)[0]


def bits_of(count):
    return list(range(count.bit_length() - 1))


def layout_kernel(x_count, raw_hbm, occupancy_hbm, exponent_hbm, *refs):
    count = WAVES * x_count
    piece_refs, left_ref = refs[:count], refs[count]
    raw_ref, occupancy_ref, exponent_ref, factor_ref, small, large = refs[count + 1 :]
    _, share, width = piece_refs[0].shape
    occupancy_copy = pltpu.make_async_copy(occupancy_hbm, occupancy_ref, small.at[0])
    exponent_copy = pltpu.make_async_copy(exponent_hbm, exponent_ref, small.at[1])
    copies = []
    for tile in range(x_count):
        rows = pl.ds(tile * share, share)
        copies.append(pltpu.make_async_copy(raw_hbm.at[:, rows], raw_ref.at[:, rows], large.at[tile]))
    occupancy_copy.start()
    exponent_copy.start()
    for copy in copies:
        copy.start()
    occupancy_copy.wait()
    exponent_copy.wait()
    for tile, copy in enumerate(copies):
        row = occupancy_ref[tile : tile + 1, :].astype(jnp.float32)
        power = jnp.exp2(jnp.broadcast_to(exponent_ref[:, tile : tile + 1], row.shape).astype(jnp.float32))
        factor = (row * power).astype(jnp.bfloat16)
        factor_ref[tile] = factor.astype(jnp.float32)
        copy.wait()
        for wave in range(WAVES):
            columns = slice(wave * width, (wave + 1) * width)
            for part in range(2):
                value = raw_ref[part, tile * share : (tile + 1) * share, columns]
                piece_refs[wave * x_count + tile][part] = value * factor[:, columns]
    col, col_count = lax.axis_index("col"), lax.axis_size("col")
    depth = raw_ref.shape[2]
    rows = raw_ref.shape[1] // col_count
    for distance in range(col_count):
        block = col ^ distance
        factor = factor_ref[block // (col_count // x_count)].astype(jnp.bfloat16)
        start = pl.multiple_of(block * rows, rows)
        for part in range(2):
            value = raw_ref[part, pl.ds(start, rows), :] * factor
            left_ref[distance * rows : (distance + 1) * rows, part * depth : (part + 1) * depth] = value


def lay_out(raw_blocks, occupancy, exponent, x_count):
    _, length, depth = raw_blocks.shape
    piece = jax.ShapeDtypeStruct((2, length // x_count, depth // WAVES), jnp.bfloat16)
    left = jax.ShapeDtypeStruct((length, 2 * depth), jnp.bfloat16)
    count = WAVES * x_count
    out = pl.pallas_call(
        functools.partial(layout_kernel, x_count),
        out_shape=[piece] * count + [left],
        in_specs=[pl.BlockSpec(memory_space=pltpu.HBM)] * 3,
        out_specs=[VMEM] * (count + 1),
        scratch_shapes=[
            pltpu.VMEM(raw_blocks.shape, jnp.bfloat16),
            pltpu.VMEM(occupancy.shape, jnp.int32),
            pltpu.VMEM(exponent.shape[::-1], jnp.int32),
            pltpu.VMEM((x_count, 1, depth), jnp.float32),
            pltpu.SemaphoreType.DMA((2,)),
            pltpu.SemaphoreType.DMA((x_count,)),
        ],
        compiler_params=PARAMS,
    )(raw_blocks, occupancy, exponent.T)
    return out[:count], out[count]


def pick_kernel(*refs):
    options, out_ref = refs[:-1], refs[-1]
    x = lax.axis_index("col") % len(options)
    for place, option_ref in enumerate(options):

        @pl.when(x == place)
        def _(option_ref=option_ref):
            out_ref[...] = option_ref[...]


def pick(options):
    return pl.pallas_call(
        pick_kernel,
        out_shape=jax.ShapeDtypeStruct(options[0].shape, options[0].dtype),
        in_specs=[VMEM] * len(options),
        out_specs=VMEM,
        compiler_params=PARAMS,
    )(*options)


def halves(blocks, bit):
    keep = [block for block in blocks if not block >> bit & 1]
    return [block | 1 << bit for block in keep], keep


def product_kernel(orders, index, mine_ref, theirs_ref, here_ref, across_ref, *refs):
    outs, slab_ref = refs[:-1], refs[-1]
    row = lax.axis_index("row")
    holds = row // 2 + row % 2 == 1
    depth, width = here_ref.shape[1:]

    def build(piece_ref):
        real, imag = piece_ref[0], piece_ref[1]
        slab_ref[:depth, :width] = real
        slab_ref[:depth, width:] = imag
        slab_ref[depth:, :width] = -imag
        slab_ref[depth:, width:] = real

    pl.when(holds)(lambda: build(here_ref))
    pl.when(jnp.logical_not(holds))(lambda: build(across_ref))
    for order, left_ref, out_ref in zip(orders, (mine_ref, theirs_ref), outs):
        count, _, rows, _ = out_ref.shape
        blocks = halves(range(2 * count), order[0])[index]
        left = jnp.concatenate([left_ref[block * rows : (block + 1) * rows, :] for block in blocks])
        value = jnp.dot(left, slab_ref[...], preferred_element_type=jnp.float32).astype(out_ref.dtype)
        for place in range(count):
            for part in range(2):
                out_ref[place, part] = value[place * rows : (place + 1) * rows, part * width : (part + 1) * width]


def products(orders, index, mine, theirs, here, across, col_count):
    out = jax.ShapeDtypeStruct((col_count // 2, 2, mine.shape[0] // col_count, here.shape[2]), jnp.bfloat16)
    return pl.pallas_call(
        functools.partial(product_kernel, orders, index),
        out_shape=[out] * 2,
        in_specs=[VMEM] * 4,
        out_specs=[VMEM] * 2,
        scratch_shapes=[pltpu.VMEM((2 * here.shape[1], 2 * here.shape[2]), jnp.bfloat16)],
        compiler_params=PARAMS,
    )(mine, theirs, here, across)


def halve_kernel(orders, step, joined, *refs):
    ins, outs = refs[:4], refs[4:]
    for chain, order in enumerate(orders):
        keep_ref, other_ref = ins[2 * chain : 2 * chain + 2]
        blocks = range(1 << len(order))
        for bit in order[:step]:
            blocks = halves(blocks, bit)[1]
        blocks = list(blocks)
        for index, kept in enumerate(halves(blocks, order[step])):
            for place, block in enumerate(kept):
                at = blocks.index(block)
                total = keep_ref[at].astype(jnp.float32) + other_ref[at].astype(jnp.float32)
                if joined:
                    outs[index][chain] = total.astype(outs[index].dtype)
                else:
                    outs[2 * chain + index][place] = total.astype(outs[2 * chain + index].dtype)


def halve(orders, step, keeps, others):
    blocks, *rest = keeps[0].shape
    joined = step == len(orders[0]) - 1 and orders[0][step] == orders[1][step]
    send = jax.ShapeDtypeStruct((2 if joined else blocks // 2, *rest), jnp.bfloat16)
    keep = jax.ShapeDtypeStruct(send.shape, jnp.float32)
    outs = pl.pallas_call(
        functools.partial(halve_kernel, orders, step, joined),
        out_shape=[send, keep] if joined else [send, keep] * 2,
        in_specs=[VMEM] * 4,
        out_specs=[VMEM] * (2 if joined else 4),
        compiler_params=PARAMS,
    )(keeps[0], others[0], keeps[1], others[1])
    return outs[0::2], outs[1::2]


def add_kernel(joined, *refs):
    ins, outs = refs[:-2], refs[-2:]
    for chain, out_ref in enumerate(outs):
        keep_ref, other_ref = ins if joined else ins[2 * chain : 2 * chain + 2]
        at = chain if joined else 0
        out_ref[...] = (keep_ref[at] + other_ref[at].astype(jnp.float32)).astype(out_ref.dtype)


def add(keeps, others):
    return pl.pallas_call(
        functools.partial(add_kernel, len(keeps) == 1),
        out_shape=[jax.ShapeDtypeStruct(keeps[0].shape[1:], jnp.bfloat16)] * 2,
        in_specs=[VMEM] * (2 * len(keeps)),
        out_specs=[VMEM] * 2,
        compiler_params=PARAMS,
    )(*[value for pair in zip(keeps, others) for value in pair])


def place_kernel(*refs):
    out_ref = refs[-1]
    core = lax.axis_index("row") % 2
    for half, panel in enumerate((core, 1 - core)):
        begin = 0
        for ref in refs[half * WAVES : (half + 1) * WAVES]:
            width = ref.shape[-1]
            out_ref[panel, :, :, begin : begin + width] = ref[...]
            begin += width


def place(own, back, depth):
    return pl.pallas_call(
        place_kernel,
        out_shape=jax.ShapeDtypeStruct((2, *own[0].shape[:-1], depth), jnp.bfloat16),
        in_specs=[VMEM] * (2 * WAVES),
        out_specs=VMEM,
        compiler_params=PARAMS,
    )(*own, *back)


def solution(mesh):
    row_count, col_count = mesh.shape["row"], mesh.shape["col"]
    x_count = col_count // row_count
    y_count = row_count // 2
    half_cols = col_count // 2
    every = range(row_count * col_count)
    x_bits = bits_of(x_count)
    z_bits = [bit for bit in bits_of(col_count) if bit not in x_bits]
    orders = (
        (x_bits + z_bits, z_bits[:1] + x_bits + z_bits[1:]),
        (x_bits + z_bits, z_bits[-1:] + x_bits + z_bits[:-1]),
    )
    steps = len(x_bits + z_bits)
    swap_core = [(r, r ^ 1) for r in range(row_count)]

    def exchange(value, bit):
        return lax.ppermute(value, "col", [(c, c ^ (1 << bit)) for c in range(col_count)])

    def filled(pairs):
        def apart(a, b):
            (row_a, col_a), (row_b, col_b) = divmod(a, col_count), divmod(b, col_count)
            far = abs(col_a // x_count - col_b // x_count) + abs(col_a % x_count - col_b % x_count)
            return 2 if a == b else 4 * far + 4 * abs(row_a // 2 - row_b // 2) + abs(row_a - row_b)

        senders = set(every) - {s for s, _ in pairs}
        receivers = set(every) - {t for _, t in pairs}
        while receivers:
            _, s, t = min((apart(s, t), s, t) for s in senders for t in receivers)
            senders.remove(s)
            receivers.remove(t)
            pairs = pairs + [(s, t)]
        return pairs

    def target(s, panel, h):
        return (2 - panel) * col_count + s * x_count + h

    def straight_pairs(h):
        return filled(
            [(s * col_count + p * half_cols, target(s, p, h)) for s in range(row_count) for p in range(2)]
        )

    def hop_pairs(h):
        return [(d, d ^ h if d % col_count % half_cols in (0, h) else d ^ col_count) for d in every]

    def spread_pairs():
        return filled(
            [
                (s * col_count + p * half_cols + h, target(s, p, h))
                for s in range(row_count)
                for p in range(2)
                for h in range(x_count)
            ]
        )

    def across_pairs():
        pairs = []
        for r in range(row_count):
            y, core = divmod(r, 2)
            pairs.append((r, r ^ 1 if y > 1 or y == core else r ^ 2))
        return pairs

    def to_all_y(here):
        across = lax.ppermute(here, "row", across_pairs())
        y = lax.axis_index("row") // 2
        if y_count > 2:
            slab = jnp.where(y + lax.axis_index("row") % 2 == 1, here, across)
            for bit in range(1, y_count.bit_length() - 1):
                got = lax.ppermute(slab, "row", [(r, r ^ (2 << bit)) for r in range(row_count)])
                slab = jnp.where((y >> bit) & 1 == 1, got, slab)
            return slab, slab
        return here, across

    def exchange_step(wave, sends, step):
        return [exchange(send, order[step]) for send, order in zip(sends, orders[wave])]

    def on_device(raw_blocks, occupancy, exponent):
        my_col = lax.axis_index("col")
        pieces, left = lay_out(raw_blocks, occupancy, exponent, x_count)

        straight = [lax.ppermute(pieces[h], ("row", "col"), straight_pairs(h)) for h in range(x_count)]
        second = pieces[x_count]
        for h in range(1, x_count):
            got = lax.ppermute(pieces[x_count + h], ("row", "col"), hop_pairs(h))
            second = jnp.where(my_col % half_cols == h, got, second)
        first = pick([after(got, second) for got in straight])
        theirs = lax.ppermute(left, "row", swap_core)

        second = lax.ppermute(second, ("row", "col"), spread_pairs())
        slabs = [to_all_y(first), to_all_y(second)]

        sends = [[], []]
        sends[0] = products(orders[0], 0, left, theirs, *slabs[0], col_count)
        others = exchange_step(0, sends[0], 0)
        keeps = products(orders[0], 1, left, theirs, *[after(slab, sends[0][0]) for slab in slabs[0]], col_count)
        sends[1] = products(orders[1], 0, left, theirs, *[after(slab, keeps[0]) for slab in slabs[1]], col_count)
        later = exchange_step(1, sends[1], 0)
        others = [after(other, sends[1][0]) for other in others]
        sends[0], keeps = halve(orders[0], 1, keeps, others)
        others = exchange_step(0, sends[0], 1)
        stay = products(orders[1], 1, left, theirs, *[after(slab, sends[0][0]) for slab in slabs[1]], col_count)
        sends[0], keeps = halve(orders[0], 2, keeps, [after(other, stay[0]) for other in others])
        others = exchange_step(0, sends[0], 2)
        for step in range(1, steps):
            if step + 1 == steps - 1:
                mine, other_rows = add(keeps, others)
                own, back = [mine], [lax.ppermute(other_rows, "row", swap_core)]
                mark = mine
            elif step + 1 < steps - 1:
                sends[0], keeps = halve(orders[0], step + 2, keeps, others)
                others = exchange_step(0, sends[0], step + 2)
                mark = sends[0][0]
            if step > 1:
                later = [after(other, mark) for other in later]
            sends[1], stay = halve(orders[1], step, stay, later)
            later = exchange_step(1, sends[1], step)
        mine, other_rows = add(stay, later)
        own.append(mine)
        back.append(lax.ppermute(other_rows, "row", swap_core))
        return place(own, back, raw_blocks.shape[2])

    placed = (P(None, "row", "col"), P("row", "col"), P("row", "col"))
    return jax.shard_map(
        on_device,
        mesh=mesh,
        in_specs=placed,
        out_specs=P(None, None, ("row", "col"), None),
        check_vma=False,
    )
```

```python
import functools

import jax
import jax.numpy as jnp
from jax import lax
from jax.experimental import pallas as pl
from jax.experimental.pallas import tpu as pltpu
from jax.sharding import PartitionSpec as P

WAVES = 2
VMEM_BYTES = 20 * 1024 * 1024
VMEM = pl.BlockSpec(memory_space=pltpu.VMEM)
PARAMS = pltpu.CompilerParams(vmem_limit_bytes=VMEM_BYTES)


def after(value, *done):
    return lax.optimization_barrier((value,) + done)[0]


def bits_of(count):
    return list(range(count.bit_length() - 1))


def column_factors(occupancy, exponent):
    power = jnp.left_shift(1, exponent + 2).astype(jnp.float32) * 0.25
    return (occupancy.astype(jnp.float32) * power).astype(jnp.bfloat16)


def layout_kernel(x_count, raw_ref, factors_ref, *refs):
    piece_refs, left_ref, factor_ref = refs[:-2], refs[-2], refs[-1]
    _, share, width = piece_refs[0].shape
    for tile in range(x_count):
        factor = factors_ref[tile : tile + 1, :]
        factor_ref[tile] = factor.astype(jnp.float32)
        for wave in range(WAVES):
            columns = slice(wave * width, (wave + 1) * width)
            for part in range(2):
                value = raw_ref[part, tile * share : (tile + 1) * share, columns]
                piece_refs[wave * x_count + tile][part] = value * factor[:, columns]
    col, col_count = lax.axis_index("col"), lax.axis_size("col")
    depth = raw_ref.shape[2]
    rows = raw_ref.shape[1] // col_count
    for distance in range(col_count):
        block = col ^ distance
        factor = factor_ref[block // (col_count // x_count)].astype(jnp.bfloat16)
        start = pl.multiple_of(block * rows, rows)
        for part in range(2):
            value = raw_ref[part, pl.ds(start, rows), :] * factor
            left_ref[distance * rows : (distance + 1) * rows, part * depth : (part + 1) * depth] = value


def lay_out(raw_blocks, factors, x_count):
    _, length, depth = raw_blocks.shape
    piece = jax.ShapeDtypeStruct((2, length // x_count, depth // WAVES), jnp.bfloat16)
    left = jax.ShapeDtypeStruct((length, 2 * depth), jnp.bfloat16)
    count = WAVES * x_count
    out = pl.pallas_call(
        functools.partial(layout_kernel, x_count),
        out_shape=[piece] * count + [left],
        in_specs=[VMEM] * 2,
        out_specs=[VMEM] * (count + 1),
        scratch_shapes=[pltpu.VMEM((x_count, 1, depth), jnp.float32)],
        compiler_params=PARAMS,
    )(raw_blocks, factors)
    return out[:count], out[count]


def pick_kernel(period, *refs):
    options, out_ref = refs[:-1], refs[-1]
    place = lax.axis_index("col") % period
    place = jnp.where(place < len(options), place, 0)
    for index, option_ref in enumerate(options):

        @pl.when(place == index)
        def _(option_ref=option_ref):
            out_ref[...] = option_ref[...]


def pick(options, period):
    return pl.pallas_call(
        functools.partial(pick_kernel, period),
        out_shape=jax.ShapeDtypeStruct(options[0].shape, options[0].dtype),
        in_specs=[VMEM] * len(options),
        out_specs=VMEM,
        compiler_params=PARAMS,
    )(*options)


def halves(blocks, bit):
    keep = [block for block in blocks if not block >> bit & 1]
    return [block | 1 << bit for block in keep], keep


def product_kernel(orders, index, mine_ref, theirs_ref, here_ref, across_ref, *refs):
    outs, slab_ref = refs[:-1], refs[-1]
    row = lax.axis_index("row")
    holds = row // 2 + row % 2 == 1
    depth, width = here_ref.shape[1:]

    def build(piece_ref):
        real, imag = piece_ref[0], piece_ref[1]
        slab_ref[:depth, :width] = real
        slab_ref[:depth, width:] = imag
        slab_ref[depth:, :width] = -imag
        slab_ref[depth:, width:] = real

    pl.when(holds)(lambda: build(here_ref))
    pl.when(jnp.logical_not(holds))(lambda: build(across_ref))
    for order, left_ref, out_ref in zip(orders, (mine_ref, theirs_ref), outs):
        count, _, rows, _ = out_ref.shape
        blocks = halves(range(2 * count), order[0])[index]
        left = jnp.concatenate([left_ref[block * rows : (block + 1) * rows, :] for block in blocks])
        value = jnp.dot(left, slab_ref[...], preferred_element_type=jnp.float32).astype(out_ref.dtype)
        for place in range(count):
            for part in range(2):
                out_ref[place, part] = value[place * rows : (place + 1) * rows, part * width : (part + 1) * width]


def products(orders, index, mine, theirs, here, across, col_count):
    out = jax.ShapeDtypeStruct((col_count // 2, 2, mine.shape[0] // col_count, here.shape[2]), jnp.bfloat16)
    return pl.pallas_call(
        functools.partial(product_kernel, orders, index),
        out_shape=[out] * 2,
        in_specs=[VMEM] * 4,
        out_specs=[VMEM] * 2,
        scratch_shapes=[pltpu.VMEM((2 * here.shape[1], 2 * here.shape[2]), jnp.bfloat16)],
        compiler_params=PARAMS,
    )(mine, theirs, here, across)


def halve_kernel(orders, step, joined, *refs):
    ins, outs = refs[:4], refs[4:]
    for chain, order in enumerate(orders):
        keep_ref, other_ref = ins[2 * chain : 2 * chain + 2]
        blocks = range(1 << len(order))
        for bit in order[:step]:
            blocks = halves(blocks, bit)[1]
        blocks = list(blocks)
        for index, kept in enumerate(halves(blocks, order[step])):
            for place, block in enumerate(kept):
                at = blocks.index(block)
                total = keep_ref[at].astype(jnp.float32) + other_ref[at].astype(jnp.float32)
                if joined:
                    outs[index][chain] = total.astype(outs[index].dtype)
                else:
                    outs[2 * chain + index][place] = total.astype(outs[2 * chain + index].dtype)


def halve(orders, step, keeps, others):
    blocks, *rest = keeps[0].shape
    joined = step == len(orders[0]) - 1 and orders[0][step] == orders[1][step]
    send = jax.ShapeDtypeStruct((2 if joined else blocks // 2, *rest), jnp.bfloat16)
    keep = jax.ShapeDtypeStruct(send.shape, jnp.float32)
    outs = pl.pallas_call(
        functools.partial(halve_kernel, orders, step, joined),
        out_shape=[send, keep] if joined else [send, keep] * 2,
        in_specs=[VMEM] * 4,
        out_specs=[VMEM] * (2 if joined else 4),
        compiler_params=PARAMS,
    )(keeps[0], others[0], keeps[1], others[1])
    return outs[0::2], outs[1::2]


def add_kernel(joined, *refs):
    ins, outs = refs[:-2], refs[-2:]
    for chain, out_ref in enumerate(outs):
        keep_ref, other_ref = ins if joined else ins[2 * chain : 2 * chain + 2]
        at = chain if joined else 0
        out_ref[...] = (keep_ref[at] + other_ref[at].astype(jnp.float32)).astype(out_ref.dtype)


def add(keeps, others):
    return pl.pallas_call(
        functools.partial(add_kernel, len(keeps) == 1),
        out_shape=[jax.ShapeDtypeStruct(keeps[0].shape[1:], jnp.bfloat16)] * 2,
        in_specs=[VMEM] * (2 * len(keeps)),
        out_specs=[VMEM] * 2,
        compiler_params=PARAMS,
    )(*[value for pair in zip(keeps, others) for value in pair])


def place_kernel(*refs):
    out_ref = refs[-1]
    core = lax.axis_index("row") % 2
    for half, panel in enumerate((core, 1 - core)):
        begin = 0
        for ref in refs[half * WAVES : (half + 1) * WAVES]:
            width = ref.shape[-1]
            out_ref[panel, :, :, begin : begin + width] = ref[...]
            begin += width


def place(own, back, depth):
    return pl.pallas_call(
        place_kernel,
        out_shape=jax.ShapeDtypeStruct((2, *own[0].shape[:-1], depth), jnp.bfloat16),
        in_specs=[VMEM] * (2 * WAVES),
        out_specs=VMEM,
        compiler_params=PARAMS,
    )(*own, *back)


def solution(mesh):
    row_count, col_count = mesh.shape["row"], mesh.shape["col"]
    x_count = col_count // row_count
    y_count = row_count // 2
    half_cols = col_count // 2
    every = range(row_count * col_count)
    x_bits = bits_of(x_count)
    z_bits = [bit for bit in bits_of(col_count) if bit not in x_bits]
    orders = (
        (x_bits + z_bits, z_bits[:1] + x_bits + z_bits[1:]),
        (x_bits + z_bits, z_bits[-1:] + x_bits + z_bits[:-1]),
    )
    steps = len(x_bits + z_bits)
    swap_core = [(r, r ^ 1) for r in range(row_count)]

    def exchange(value, bit):
        return lax.ppermute(value, "col", [(c, c ^ (1 << bit)) for c in range(col_count)])

    def filled(pairs):
        def apart(a, b):
            (row_a, col_a), (row_b, col_b) = divmod(a, col_count), divmod(b, col_count)
            far = abs(col_a // x_count - col_b // x_count) + abs(col_a % x_count - col_b % x_count)
            return 2 if a == b else 4 * far + 4 * abs(row_a // 2 - row_b // 2) + abs(row_a - row_b)

        senders = set(every) - {s for s, _ in pairs}
        receivers = set(every) - {t for _, t in pairs}
        while receivers:
            _, s, t = min((apart(s, t), s, t) for s in senders for t in receivers)
            senders.remove(s)
            receivers.remove(t)
            pairs = pairs + [(s, t)]
        return pairs

    def target(s, panel, h):
        return (2 - panel) * col_count + s * x_count + h

    def straight_pairs(h):
        return filled(
            [(s * col_count + p * half_cols, target(s, p, h)) for s in range(row_count) for p in range(2)]
        )

    def hop_pairs(h):
        return [(d, d ^ h if d % col_count % half_cols in (0, h) else d ^ col_count) for d in every]

    def spread_pairs():
        return filled(
            [
                (s * col_count + p * half_cols + h, target(s, p, h))
                for s in range(row_count)
                for p in range(2)
                for h in range(x_count)
            ]
        )

    def across_pairs():
        pairs = []
        for r in range(row_count):
            y, core = divmod(r, 2)
            pairs.append((r, r ^ 1 if y > 1 or y == core else r ^ 2))
        return pairs

    def to_all_y(here):
        across = lax.ppermute(here, "row", across_pairs())
        y = lax.axis_index("row") // 2
        if y_count > 2:
            slab = jnp.where(y + lax.axis_index("row") % 2 == 1, here, across)
            for bit in range(1, y_count.bit_length() - 1):
                got = lax.ppermute(slab, "row", [(r, r ^ (2 << bit)) for r in range(row_count)])
                slab = jnp.where((y >> bit) & 1 == 1, got, slab)
            return slab, slab
        return here, across

    def exchange_step(wave, sends, step):
        return [exchange(send, order[step]) for send, order in zip(sends, orders[wave])]

    def on_device(raw_blocks, occupancy, exponent):
        pieces, left = lay_out(raw_blocks, column_factors(occupancy, exponent), x_count)

        straight = [lax.ppermute(pieces[h], ("row", "col"), straight_pairs(h)) for h in range(x_count)]
        hopped = [pieces[x_count]]
        for h in range(1, x_count):
            hopped.append(lax.ppermute(pieces[x_count + h], ("row", "col"), hop_pairs(h)))
        second = pick(hopped, half_cols)
        first = pick([after(got, second) for got in straight], x_count)
        theirs = lax.ppermute(left, "row", swap_core)

        second = lax.ppermute(second, ("row", "col"), spread_pairs())
        slabs = [to_all_y(first), to_all_y(second)]

        sends = [[], []]
        sends[0] = products(orders[0], 0, left, theirs, *slabs[0], col_count)
        others = exchange_step(0, sends[0], 0)
        keeps = products(orders[0], 1, left, theirs, *[after(slab, sends[0][0]) for slab in slabs[0]], col_count)
        sends[1] = products(orders[1], 0, left, theirs, *[after(slab, keeps[0]) for slab in slabs[1]], col_count)
        later = exchange_step(1, sends[1], 0)
        others = [after(other, sends[1][0]) for other in others]
        sends[0], keeps = halve(orders[0], 1, keeps, others)
        others = exchange_step(0, sends[0], 1)
        stay = products(orders[1], 1, left, theirs, *[after(slab, sends[0][0]) for slab in slabs[1]], col_count)
        sends[0], keeps = halve(orders[0], 2, keeps, [after(other, stay[0]) for other in others])
        others = exchange_step(0, sends[0], 2)
        for step in range(1, steps):
            if step + 1 == steps - 1:
                mine, other_rows = add(keeps, others)
                own, back = [mine], [lax.ppermute(other_rows, "row", swap_core)]
                mark = mine
            elif step + 1 < steps - 1:
                sends[0], keeps = halve(orders[0], step + 2, keeps, others)
                others = exchange_step(0, sends[0], step + 2)
                mark = sends[0][0]
            if step > 1:
                later = [after(other, mark) for other in later]
            sends[1], stay = halve(orders[1], step, stay, later)
            later = exchange_step(1, sends[1], step)
        mine, other_rows = add(stay, later)
        own.append(mine)
        back.append(lax.ppermute(other_rows, "row", swap_core))
        return place(own, back, raw_blocks.shape[2])

    placed = (P(None, "row", "col"), P("row", "col"), P("row", "col"))
    return jax.shard_map(
        on_device,
        mesh=mesh,
        in_specs=placed,
        out_specs=P(None, None, ("row", "col"), None),
        check_vma=False,
    )
```

```python
import functools

import jax
import jax.numpy as jnp
from jax import lax
from jax.experimental import pallas as pl
from jax.experimental.pallas import tpu as pltpu
from jax.sharding import PartitionSpec as P

WAVES = 2
VMEM_BYTES = 20 * 1024 * 1024
VMEM = pl.BlockSpec(memory_space=pltpu.VMEM)
PARAMS = pltpu.CompilerParams(vmem_limit_bytes=VMEM_BYTES)


def after(value, *done):
    return lax.optimization_barrier((value,) + done)[0]


def bits_of(count):
    return list(range(count.bit_length() - 1))


def column_factors(occupancy, exponent):
    power = jnp.left_shift(1, exponent + 2).astype(jnp.float32) * 0.25
    return (occupancy.astype(jnp.float32) * power).astype(jnp.bfloat16)


def layout_kernel(x_count, raw_ref, factors_ref, *refs):
    piece_refs, left_ref, factor_ref = refs[:-2], refs[-2], refs[-1]
    _, share, width = piece_refs[0].shape
    for tile in range(x_count):
        factor = factors_ref[tile : tile + 1, :]
        factor_ref[tile] = factor.astype(jnp.float32)
        for wave in range(WAVES):
            columns = slice(wave * width, (wave + 1) * width)
            for part in range(2):
                value = raw_ref[part, tile * share : (tile + 1) * share, columns]
                piece_refs[wave * x_count + tile][part] = value * factor[:, columns]
    col, col_count = lax.axis_index("col"), lax.axis_size("col")
    depth = raw_ref.shape[2]
    rows = raw_ref.shape[1] // col_count
    for distance in range(col_count):
        block = col ^ distance
        factor = factor_ref[block // (col_count // x_count)].astype(jnp.bfloat16)
        start = pl.multiple_of(block * rows, rows)
        for part in range(2):
            value = raw_ref[part, pl.ds(start, rows), :] * factor
            left_ref[distance * rows : (distance + 1) * rows, part * depth : (part + 1) * depth] = value


def lay_out(raw_blocks, factors, x_count):
    _, length, depth = raw_blocks.shape
    piece = jax.ShapeDtypeStruct((2, length // x_count, depth // WAVES), jnp.bfloat16)
    left = jax.ShapeDtypeStruct((length, 2 * depth), jnp.bfloat16)
    count = WAVES * x_count
    out = pl.pallas_call(
        functools.partial(layout_kernel, x_count),
        out_shape=[piece] * count + [left],
        in_specs=[VMEM] * 2,
        out_specs=[VMEM] * (count + 1),
        scratch_shapes=[pltpu.VMEM((x_count, 1, depth), jnp.float32)],
        compiler_params=PARAMS,
    )(raw_blocks, factors)
    return out[:count], out[count]


def pick_kernel(period, *refs):
    options, out_ref = refs[:-1], refs[-1]
    place = lax.axis_index("col") % period
    place = jnp.where(place < len(options), place, 0)
    for index, option_ref in enumerate(options):

        @pl.when(place == index)
        def _(option_ref=option_ref):
            out_ref[...] = option_ref[...]


def pick(options, period):
    return pl.pallas_call(
        functools.partial(pick_kernel, period),
        out_shape=jax.ShapeDtypeStruct(options[0].shape, options[0].dtype),
        in_specs=[VMEM] * len(options),
        out_specs=VMEM,
        compiler_params=PARAMS,
    )(*options)


def halves(blocks, bit):
    keep = [block for block in blocks if not block >> bit & 1]
    return [block | 1 << bit for block in keep], keep


def product_kernel(orders, index, mine_ref, theirs_ref, here_ref, across_ref, *refs):
    outs, slab_ref = refs[:-1], refs[-1]
    row = lax.axis_index("row")
    holds = row // 2 + row % 2 == 1
    depth, width = here_ref.shape[1:]

    def build(piece_ref):
        real, imag = piece_ref[0], piece_ref[1]
        slab_ref[:depth, :width] = real
        slab_ref[:depth, width:] = imag
        slab_ref[depth:, :width] = -imag
        slab_ref[depth:, width:] = real

    pl.when(holds)(lambda: build(here_ref))
    pl.when(jnp.logical_not(holds))(lambda: build(across_ref))
    for order, left_ref, out_ref in zip(orders, (mine_ref, theirs_ref), outs):
        count, _, rows, _ = out_ref.shape
        blocks = halves(range(2 * count), order[0])[index]
        left = jnp.concatenate([left_ref[block * rows : (block + 1) * rows, :] for block in blocks])
        value = jnp.dot(left, slab_ref[...], preferred_element_type=jnp.float32).astype(out_ref.dtype)
        for place in range(count):
            for part in range(2):
                out_ref[place, part] = value[place * rows : (place + 1) * rows, part * width : (part + 1) * width]


def products(orders, index, mine, theirs, here, across, col_count):
    out = jax.ShapeDtypeStruct((col_count // 2, 2, mine.shape[0] // col_count, here.shape[2]), jnp.bfloat16)
    return pl.pallas_call(
        functools.partial(product_kernel, orders, index),
        out_shape=[out] * 2,
        in_specs=[VMEM] * 4,
        out_specs=[VMEM] * 2,
        scratch_shapes=[pltpu.VMEM((2 * here.shape[1], 2 * here.shape[2]), jnp.bfloat16)],
        compiler_params=PARAMS,
    )(mine, theirs, here, across)


def halve_kernel(orders, step, joined, *refs):
    ins, outs = refs[:4], refs[4:]
    for chain, order in enumerate(orders):
        keep_ref, other_ref = ins[2 * chain : 2 * chain + 2]
        blocks = range(1 << len(order))
        for bit in order[:step]:
            blocks = halves(blocks, bit)[1]
        blocks = list(blocks)
        for index, kept in enumerate(halves(blocks, order[step])):
            for place, block in enumerate(kept):
                at = blocks.index(block)
                total = keep_ref[at].astype(jnp.float32) + other_ref[at].astype(jnp.float32)
                if joined:
                    outs[index][chain] = total.astype(outs[index].dtype)
                else:
                    outs[2 * chain + index][place] = total.astype(outs[2 * chain + index].dtype)


def halve(orders, step, keeps, others):
    blocks, *rest = keeps[0].shape
    last = step == len(orders[0]) - 1
    joined = last and orders[0][step] == orders[1][step]
    send = jax.ShapeDtypeStruct((2 if joined else blocks // 2, *rest), jnp.bfloat16)
    keep = jax.ShapeDtypeStruct(send.shape, jnp.float32)
    outs = pl.pallas_call(
        functools.partial(halve_kernel, orders, step, joined),
        out_shape=[send, keep] if joined else [send, keep, send, send if last else keep],
        in_specs=[VMEM] * 4,
        out_specs=[VMEM] * (2 if joined else 4),
        compiler_params=PARAMS,
    )(keeps[0], others[0], keeps[1], others[1])
    return outs[0::2], outs[1::2]


def add_kernel(joined, *refs):
    ins, outs = refs[:-2], refs[-2:]
    for chain, out_ref in enumerate(outs):
        keep_ref, other_ref = ins if joined else ins[2 * chain : 2 * chain + 2]
        at = chain if joined else 0
        out_ref[...] = (keep_ref[at] + other_ref[at].astype(jnp.float32)).astype(out_ref.dtype)


def add(keeps, others):
    return pl.pallas_call(
        functools.partial(add_kernel, len(keeps) == 1),
        out_shape=[jax.ShapeDtypeStruct(keeps[0].shape[1:], jnp.bfloat16)] * 2,
        in_specs=[VMEM] * (2 * len(keeps)),
        out_specs=[VMEM] * 2,
        compiler_params=PARAMS,
    )(*[value for pair in zip(keeps, others) for value in pair])


def finish_kernel(mine_ref, back_ref, *refs):
    parts, out_ref = refs[:-1], refs[-1]
    core = lax.axis_index("row") % 2
    width = mine_ref.shape[-1]
    for chain, (panel, ready_ref) in enumerate(((core, mine_ref), (1 - core, back_ref))):
        out_ref[panel, :, :, :width] = ready_ref[...]
        total = parts[2 * chain][0].astype(jnp.float32) + parts[2 * chain + 1][0].astype(jnp.float32)
        out_ref[panel, :, :, width:] = total.astype(out_ref.dtype)


def finish(mine, back, *parts):
    width = mine.shape[-1] + parts[0].shape[-1]
    return pl.pallas_call(
        finish_kernel,
        out_shape=jax.ShapeDtypeStruct((2, *mine.shape[:-1], width), jnp.bfloat16),
        in_specs=[VMEM] * (2 + len(parts)),
        out_specs=VMEM,
        compiler_params=PARAMS,
    )(mine, back, *parts)


def solution(mesh):
    row_count, col_count = mesh.shape["row"], mesh.shape["col"]
    x_count = col_count // row_count
    y_count = row_count // 2
    half_cols = col_count // 2
    every = range(row_count * col_count)
    x_bits = bits_of(x_count)
    z_bits = [bit for bit in bits_of(col_count) if bit not in x_bits]
    orders = (
        (x_bits + z_bits, z_bits[:1] + x_bits + z_bits[1:]),
        (x_bits + z_bits, z_bits[-1:] + x_bits + z_bits[:-1]),
    )
    steps = len(x_bits + z_bits)
    swap_core = [(r, r ^ 1) for r in range(row_count)]

    def exchange(value, bit):
        return lax.ppermute(value, "col", [(c, c ^ (1 << bit)) for c in range(col_count)])

    def filled(pairs):
        def apart(a, b):
            (row_a, col_a), (row_b, col_b) = divmod(a, col_count), divmod(b, col_count)
            far = abs(col_a // x_count - col_b // x_count) + abs(col_a % x_count - col_b % x_count)
            return 2 if a == b else 4 * far + 4 * abs(row_a // 2 - row_b // 2) + abs(row_a - row_b)

        senders = set(every) - {s for s, _ in pairs}
        receivers = set(every) - {t for _, t in pairs}
        while receivers:
            _, s, t = min((apart(s, t), s, t) for s in senders for t in receivers)
            senders.remove(s)
            receivers.remove(t)
            pairs = pairs + [(s, t)]
        return pairs

    def target(s, panel, h):
        return (2 - panel) * col_count + s * x_count + h

    def straight_pairs(h):
        return filled(
            [(s * col_count + p * half_cols, target(s, p, h)) for s in range(row_count) for p in range(2)]
        )

    def hop_pairs(h):
        return [(d, d ^ h if d % col_count % half_cols in (0, h) else d ^ col_count) for d in every]

    def spread_pairs():
        return filled(
            [
                (s * col_count + p * half_cols + h, target(s, p, h))
                for s in range(row_count)
                for p in range(2)
                for h in range(x_count)
            ]
        )

    def across_pairs():
        pairs = []
        for r in range(row_count):
            y, core = divmod(r, 2)
            pairs.append((r, r ^ 1 if y > 1 or y == core else r ^ 2))
        return pairs

    def to_all_y(here):
        across = lax.ppermute(here, "row", across_pairs())
        y = lax.axis_index("row") // 2
        if y_count > 2:
            slab = jnp.where(y + lax.axis_index("row") % 2 == 1, here, across)
            for bit in range(1, y_count.bit_length() - 1):
                got = lax.ppermute(slab, "row", [(r, r ^ (2 << bit)) for r in range(row_count)])
                slab = jnp.where((y >> bit) & 1 == 1, got, slab)
            return slab, slab
        return here, across

    def exchange_step(wave, sends, step):
        return [exchange(send, order[step]) for send, order in zip(sends, orders[wave])]

    def on_device(raw_blocks, occupancy, exponent):
        pieces, left = lay_out(raw_blocks, column_factors(occupancy, exponent), x_count)

        straight = [lax.ppermute(pieces[h], ("row", "col"), straight_pairs(h)) for h in range(x_count)]
        hopped = [pieces[x_count]]
        for h in range(1, x_count):
            hopped.append(lax.ppermute(pieces[x_count + h], ("row", "col"), hop_pairs(h)))
        second = pick(hopped, half_cols)
        first = pick([after(got, second) for got in straight], x_count)
        theirs = lax.ppermute(left, "row", swap_core)

        second = lax.ppermute(second, ("row", "col"), spread_pairs())
        slabs = [to_all_y(first), to_all_y(second)]

        sends = [[], []]
        sends[0] = products(orders[0], 0, left, theirs, *slabs[0], col_count)
        others = exchange_step(0, sends[0], 0)
        keeps = products(orders[0], 1, left, theirs, *[after(slab, sends[0][0]) for slab in slabs[0]], col_count)
        sends[1] = products(orders[1], 0, left, theirs, *[after(slab, keeps[0]) for slab in slabs[1]], col_count)
        later = exchange_step(1, sends[1], 0)
        others = [after(other, sends[1][0]) for other in others]
        sends[0], keeps = halve(orders[0], 1, keeps, others)
        others = exchange_step(0, sends[0], 1)
        stay = products(orders[1], 1, left, theirs, *[after(slab, sends[0][0]) for slab in slabs[1]], col_count)
        sends[0], keeps = halve(orders[0], 2, keeps, [after(other, stay[0]) for other in others])
        others = exchange_step(0, sends[0], 2)
        for step in range(1, steps):
            if step + 1 == steps - 1:
                mine, other_rows = add(keeps, others)
                back = lax.ppermute(other_rows, "row", swap_core)
                mark = mine
            elif step + 1 < steps - 1:
                sends[0], keeps = halve(orders[0], step + 2, keeps, others)
                others = exchange_step(0, sends[0], step + 2)
                mark = sends[0][0]
            if step > 1:
                later = [after(other, mark) for other in later]
            sends[1], stay = halve(orders[1], step, stay, later)
            if step < steps - 1:
                later = exchange_step(1, sends[1], step)
        near = exchange(sends[1][0], orders[1][0][-1])
        across = [(d, d ^ col_count ^ (1 << orders[1][1][-1])) for d in every]
        far = lax.ppermute(sends[1][1], ("row", "col"), across)
        kept = lax.ppermute(stay[1], "row", swap_core)
        return finish(mine, back, stay[0], near, kept, far)

    placed = (P(None, "row", "col"), P("row", "col"), P("row", "col"))
    return jax.shard_map(
        on_device,
        mesh=mesh,
        in_specs=placed,
        out_specs=P(None, None, ("row", "col"), None),
        check_vma=False,
    )
```

```python
import functools

import jax
import jax.numpy as jnp
from jax import lax
from jax.experimental import pallas as pl
from jax.experimental.pallas import tpu as pltpu
from jax.sharding import PartitionSpec as P

WAVES = 2
VMEM_BYTES = 20 * 1024 * 1024
VMEM = pl.BlockSpec(memory_space=pltpu.VMEM)
PARAMS = pltpu.CompilerParams(vmem_limit_bytes=VMEM_BYTES)


def after(value, *done):
    return lax.optimization_barrier((value,) + done)[0]


def bits_of(count):
    return list(range(count.bit_length() - 1))


def column_factors(occupancy, exponent):
    power = jnp.left_shift(1, exponent + 2).astype(jnp.float32) * 0.25
    return (occupancy.astype(jnp.float32) * power).astype(jnp.bfloat16)


def layout_kernel(x_count, raw_ref, factors_ref, *refs):
    piece_refs, left_ref, factor_ref = refs[:-2], refs[-2], refs[-1]
    _, share, width = piece_refs[0].shape
    for tile in range(x_count):
        factor = factors_ref[tile : tile + 1, :]
        factor_ref[tile] = factor.astype(jnp.float32)
        for wave in range(WAVES):
            columns = slice(wave * width, (wave + 1) * width)
            for part in range(2):
                value = raw_ref[part, tile * share : (tile + 1) * share, columns]
                piece_refs[wave * x_count + tile][part] = value * factor[:, columns]
    col, col_count = lax.axis_index("col"), lax.axis_size("col")
    depth = raw_ref.shape[2]
    rows = raw_ref.shape[1] // col_count
    for distance in range(col_count):
        block = col ^ distance
        factor = factor_ref[block // (col_count // x_count)].astype(jnp.bfloat16)
        start = pl.multiple_of(block * rows, rows)
        for part in range(2):
            value = raw_ref[part, pl.ds(start, rows), :] * factor
            left_ref[distance * rows : (distance + 1) * rows, part * depth : (part + 1) * depth] = value


def lay_out(raw_blocks, factors, x_count):
    _, length, depth = raw_blocks.shape
    piece = jax.ShapeDtypeStruct((2, length // x_count, depth // WAVES), jnp.bfloat16)
    left = jax.ShapeDtypeStruct((length, 2 * depth), jnp.bfloat16)
    count = WAVES * x_count
    out = pl.pallas_call(
        functools.partial(layout_kernel, x_count),
        out_shape=[piece] * count + [left],
        in_specs=[VMEM] * 2,
        out_specs=[VMEM] * (count + 1),
        scratch_shapes=[pltpu.VMEM((x_count, 1, depth), jnp.float32)],
        compiler_params=PARAMS,
    )(raw_blocks, factors)
    return out[:count], out[count]


def pick_kernel(period, *refs):
    options, out_ref = refs[:-1], refs[-1]
    place = lax.axis_index("col") % period
    place = jnp.where(place < len(options), place, 0)
    for index, option_ref in enumerate(options):

        @pl.when(place == index)
        def _(option_ref=option_ref):
            out_ref[...] = option_ref[...]


def pick(options, period):
    return pl.pallas_call(
        functools.partial(pick_kernel, period),
        out_shape=jax.ShapeDtypeStruct(options[0].shape, options[0].dtype),
        in_specs=[VMEM] * len(options),
        out_specs=VMEM,
        compiler_params=PARAMS,
    )(*options)


def halves(blocks, bit):
    keep = [block for block in blocks if not block >> bit & 1]
    return [block | 1 << bit for block in keep], keep


def product_kernel(orders, index, mine_ref, theirs_ref, here_ref, across_ref, *refs):
    outs, slab_ref = refs[:-1], refs[-1]
    row = lax.axis_index("row")
    holds = row // 2 + row % 2 == 1
    depth, width = here_ref.shape[1:]

    def build(piece_ref):
        real, imag = piece_ref[0], piece_ref[1]
        slab_ref[:depth, :width] = real
        slab_ref[:depth, width:] = imag
        slab_ref[depth:, :width] = -imag
        slab_ref[depth:, width:] = real

    pl.when(holds)(lambda: build(here_ref))
    pl.when(jnp.logical_not(holds))(lambda: build(across_ref))
    for order, left_ref, out_ref in zip(orders, (mine_ref, theirs_ref), outs):
        count, _, rows, _ = out_ref.shape
        blocks = halves(range(2 * count), order[0])[index]
        left = jnp.concatenate([left_ref[block * rows : (block + 1) * rows, :] for block in blocks])
        value = jnp.dot(left, slab_ref[...], preferred_element_type=jnp.float32).astype(out_ref.dtype)
        for place in range(count):
            for part in range(2):
                out_ref[place, part] = value[place * rows : (place + 1) * rows, part * width : (part + 1) * width]


def products(orders, index, mine, theirs, here, across, col_count):
    out = jax.ShapeDtypeStruct((col_count // 2, 2, mine.shape[0] // col_count, here.shape[2]), jnp.bfloat16)
    return pl.pallas_call(
        functools.partial(product_kernel, orders, index),
        out_shape=[out] * 2,
        in_specs=[VMEM] * 4,
        out_specs=[VMEM] * 2,
        scratch_shapes=[pltpu.VMEM((2 * here.shape[1], 2 * here.shape[2]), jnp.bfloat16)],
        compiler_params=PARAMS,
    )(mine, theirs, here, across)


def halve_kernel(orders, step, joined, *refs):
    ins, refs = refs[:4], refs[4:]
    outs = refs[-2:] if joined else refs[-4:]
    for chain, order in enumerate(orders):
        keep_ref, other_ref = ins[2 * chain : 2 * chain + 2]
        blocks = range(1 << len(order))
        for bit in order[:step]:
            blocks = halves(blocks, bit)[1]
        blocks = list(blocks)
        for index, kept in enumerate(halves(blocks, order[step])):
            for place, block in enumerate(kept):
                at = blocks.index(block)
                total = keep_ref[at].astype(jnp.float32) + other_ref[at].astype(jnp.float32)
                if joined:
                    outs[index][chain] = total.astype(outs[index].dtype)
                else:
                    out_ref = outs[2 * chain + index]
                    out_ref[out_ref.shape[0] - len(kept) + place] = total.astype(out_ref.dtype)
    if len(refs) > len(outs):
        outs[3][0] = refs[0][...]


def halve(orders, step, keeps, others, ready=None):
    blocks, *rest = keeps[0].shape
    last = step == len(orders[0]) - 1
    joined = last and orders[0][step] == orders[1][step]
    send = jax.ShapeDtypeStruct((2 if joined else blocks // 2, *rest), jnp.bfloat16)
    keep = jax.ShapeDtypeStruct(send.shape, jnp.float32)
    moving = jax.ShapeDtypeStruct((2, *rest), jnp.bfloat16)
    outs = pl.pallas_call(
        functools.partial(halve_kernel, orders, step, joined),
        out_shape=[send, keep] if joined else [send, keep, send, keep if ready is None else moving],
        in_specs=[VMEM] * (4 if ready is None else 5),
        out_specs=[VMEM] * (2 if joined else 4),
        compiler_params=PARAMS,
    )(keeps[0], others[0], keeps[1], others[1], *(() if ready is None else (ready,)))
    return outs[0::2], outs[1::2]


def add_kernel(joined, *refs):
    ins, outs = refs[:-2], refs[-2:]
    for chain, out_ref in enumerate(outs):
        keep_ref, other_ref = ins if joined else ins[2 * chain : 2 * chain + 2]
        at = chain if joined else 0
        out_ref[...] = (keep_ref[at] + other_ref[at].astype(jnp.float32)).astype(out_ref.dtype)


def add(keeps, others):
    return pl.pallas_call(
        functools.partial(add_kernel, len(keeps) == 1),
        out_shape=[jax.ShapeDtypeStruct(keeps[0].shape[1:], jnp.bfloat16)] * 2,
        in_specs=[VMEM] * (2 * len(keeps)),
        out_specs=[VMEM] * 2,
        compiler_params=PARAMS,
    )(*[value for pair in zip(keeps, others) for value in pair])


def finish_kernel(mine_ref, keep_ref, near_ref, moved_ref, far_ref, out_ref):
    core = lax.axis_index("row") % 2
    width = mine_ref.shape[-1]
    out_ref[core, :, :, :width] = mine_ref[...]
    out_ref[core, :, :, width:] = (keep_ref[0] + near_ref[0].astype(jnp.float32)).astype(out_ref.dtype)
    out_ref[1 - core, :, :, :width] = moved_ref[0]
    total = moved_ref[1].astype(jnp.float32) + far_ref[0].astype(jnp.float32)
    out_ref[1 - core, :, :, width:] = total.astype(out_ref.dtype)


def finish(mine, *parts):
    width = mine.shape[-1] + parts[0].shape[-1]
    return pl.pallas_call(
        finish_kernel,
        out_shape=jax.ShapeDtypeStruct((2, *mine.shape[:-1], width), jnp.bfloat16),
        in_specs=[VMEM] * (1 + len(parts)),
        out_specs=VMEM,
        compiler_params=PARAMS,
    )(mine, *parts)


def solution(mesh):
    row_count, col_count = mesh.shape["row"], mesh.shape["col"]
    x_count = col_count // row_count
    y_count = row_count // 2
    half_cols = col_count // 2
    every = range(row_count * col_count)
    x_bits = bits_of(x_count)
    z_bits = [bit for bit in bits_of(col_count) if bit not in x_bits]
    orders = (
        (x_bits + z_bits, z_bits[:1] + x_bits + z_bits[1:]),
        (x_bits + z_bits, z_bits[-1:] + x_bits + z_bits[:-1]),
    )
    steps = len(x_bits + z_bits)
    swap_core = [(r, r ^ 1) for r in range(row_count)]

    def exchange(value, bit):
        return lax.ppermute(value, "col", [(c, c ^ (1 << bit)) for c in range(col_count)])

    def filled(pairs):
        def apart(a, b):
            (row_a, col_a), (row_b, col_b) = divmod(a, col_count), divmod(b, col_count)
            far = abs(col_a // x_count - col_b // x_count) + abs(col_a % x_count - col_b % x_count)
            return 2 if a == b else 4 * far + 4 * abs(row_a // 2 - row_b // 2) + abs(row_a - row_b)

        senders = set(every) - {s for s, _ in pairs}
        receivers = set(every) - {t for _, t in pairs}
        while receivers:
            _, s, t = min((apart(s, t), s, t) for s in senders for t in receivers)
            senders.remove(s)
            receivers.remove(t)
            pairs = pairs + [(s, t)]
        return pairs

    def target(s, panel, h):
        return (2 - panel) * col_count + s * x_count + h

    def straight_pairs(h):
        return filled(
            [(s * col_count + p * half_cols, target(s, p, h)) for s in range(row_count) for p in range(2)]
        )

    def hop_pairs(h):
        return [(d, d ^ h if d % col_count % half_cols in (0, h) else d ^ col_count) for d in every]

    def spread_pairs():
        return filled(
            [
                (s * col_count + p * half_cols + h, target(s, p, h))
                for s in range(row_count)
                for p in range(2)
                for h in range(x_count)
            ]
        )

    def across_pairs():
        pairs = []
        for r in range(row_count):
            y, core = divmod(r, 2)
            pairs.append((r, r ^ 1 if y > 1 or y == core else r ^ 2))
        return pairs

    def to_all_y(here):
        across = lax.ppermute(here, "row", across_pairs())
        y = lax.axis_index("row") // 2
        if y_count > 2:
            slab = jnp.where(y + lax.axis_index("row") % 2 == 1, here, across)
            for bit in range(1, y_count.bit_length() - 1):
                got = lax.ppermute(slab, "row", [(r, r ^ (2 << bit)) for r in range(row_count)])
                slab = jnp.where((y >> bit) & 1 == 1, got, slab)
            return slab, slab
        return here, across

    def exchange_step(wave, sends, step):
        return [exchange(send, order[step]) for send, order in zip(sends, orders[wave])]

    def on_device(raw_blocks, occupancy, exponent):
        pieces, left = lay_out(raw_blocks, column_factors(occupancy, exponent), x_count)

        straight = [lax.ppermute(pieces[h], ("row", "col"), straight_pairs(h)) for h in range(x_count)]
        hopped = [pieces[x_count]]
        for h in range(1, x_count):
            hopped.append(lax.ppermute(pieces[x_count + h], ("row", "col"), hop_pairs(h)))
        second = pick(hopped, half_cols)
        first = pick([after(got, second) for got in straight], x_count)
        theirs = lax.ppermute(left, "row", swap_core)

        second = lax.ppermute(second, ("row", "col"), spread_pairs())
        slabs = [to_all_y(first), to_all_y(second)]

        sends = [[], []]
        sends[0] = products(orders[0], 0, left, theirs, *slabs[0], col_count)
        others = exchange_step(0, sends[0], 0)
        keeps = products(orders[0], 1, left, theirs, *[after(slab, sends[0][0]) for slab in slabs[0]], col_count)
        sends[1] = products(orders[1], 0, left, theirs, *[after(slab, keeps[0]) for slab in slabs[1]], col_count)
        later = exchange_step(1, sends[1], 0)
        others = [after(other, sends[1][0]) for other in others]
        sends[0], keeps = halve(orders[0], 1, keeps, others)
        others = exchange_step(0, sends[0], 1)
        stay = products(orders[1], 1, left, theirs, *[after(slab, sends[0][0]) for slab in slabs[1]], col_count)
        sends[0], keeps = halve(orders[0], 2, keeps, [after(other, stay[0]) for other in others])
        others = exchange_step(0, sends[0], 2)
        for step in range(1, steps):
            if step + 1 == steps - 1:
                mine, other_rows = add(keeps, others)
                mark = mine
            elif step + 1 < steps - 1:
                sends[0], keeps = halve(orders[0], step + 2, keeps, others)
                others = exchange_step(0, sends[0], step + 2)
                mark = sends[0][0]
            if step > 1:
                later = [after(other, mark) for other in later]
            sends[1], stay = halve(orders[1], step, stay, later, other_rows if step == steps - 1 else None)
            if step < steps - 1:
                later = exchange_step(1, sends[1], step)
        near = exchange(sends[1][0], orders[1][0][-1])
        across = [(d, d ^ col_count ^ (1 << orders[1][1][-1])) for d in every]
        far = lax.ppermute(sends[1][1], ("row", "col"), across)
        moved = lax.ppermute(stay[1], "row", swap_core)
        return finish(mine, stay[0], near, moved, far)

    placed = (P(None, "row", "col"), P("row", "col"), P("row", "col"))
    return jax.shard_map(
        on_device,
        mesh=mesh,
        in_specs=placed,
        out_specs=P(None, None, ("row", "col"), None),
        check_vma=False,
    )
```

```python
import functools

import jax
import jax.numpy as jnp
from jax import lax
from jax.experimental import pallas as pl
from jax.experimental.pallas import tpu as pltpu
from jax.sharding import PartitionSpec as P

WAVES = 2
VMEM_BYTES = 20 * 1024 * 1024
VMEM = pl.BlockSpec(memory_space=pltpu.VMEM)
PARAMS = pltpu.CompilerParams(vmem_limit_bytes=VMEM_BYTES)


def after(value, *done):
    return lax.optimization_barrier((value,) + done)[0]


def bits_of(count):
    return list(range(count.bit_length() - 1))


def column_factors(occupancy, exponent):
    places = jnp.maximum(jnp.broadcast_to(exponent, occupancy.shape) + 2 * occupancy, 0)
    return (jnp.left_shift(occupancy, places).astype(jnp.float32) * 0.25).astype(jnp.bfloat16)


def layout_kernel(x_count, raw_ref, factors_ref, *refs):
    piece_refs, left_ref, factor_ref = refs[:-2], refs[-2], refs[-1]
    _, share, width = piece_refs[0].shape
    for tile in range(x_count):
        factor = factors_ref[tile : tile + 1, :]
        factor_ref[tile] = factor.astype(jnp.float32)
        for wave in range(WAVES):
            columns = slice(wave * width, (wave + 1) * width)
            for part in range(2):
                value = raw_ref[part, tile * share : (tile + 1) * share, columns]
                piece_refs[wave * x_count + tile][part] = value * factor[:, columns]
    col, col_count = lax.axis_index("col"), lax.axis_size("col")
    depth = raw_ref.shape[2]
    rows = raw_ref.shape[1] // col_count
    for distance in range(col_count):
        block = col ^ distance
        factor = factor_ref[block // (col_count // x_count)].astype(jnp.bfloat16)
        start = pl.multiple_of(block * rows, rows)
        for part in range(2):
            value = raw_ref[part, pl.ds(start, rows), :] * factor
            left_ref[distance * rows : (distance + 1) * rows, part * depth : (part + 1) * depth] = value


def lay_out(raw_blocks, factors, x_count):
    _, length, depth = raw_blocks.shape
    piece = jax.ShapeDtypeStruct((2, length // x_count, depth // WAVES), jnp.bfloat16)
    left = jax.ShapeDtypeStruct((length, 2 * depth), jnp.bfloat16)
    count = WAVES * x_count
    out = pl.pallas_call(
        functools.partial(layout_kernel, x_count),
        out_shape=[piece] * count + [left],
        in_specs=[VMEM] * 2,
        out_specs=[VMEM] * (count + 1),
        scratch_shapes=[pltpu.VMEM((x_count, 1, depth), jnp.float32)],
        compiler_params=PARAMS,
    )(raw_blocks, factors)
    return out[:count], out[count]


def pick_kernel(period, *refs):
    options, out_ref = refs[:-1], refs[-1]
    place = lax.axis_index("col") % period
    place = jnp.where(place < len(options), place, 0)
    for index, option_ref in enumerate(options):

        @pl.when(place == index)
        def _(option_ref=option_ref):
            out_ref[...] = option_ref[...]


def pick(options, period):
    return pl.pallas_call(
        functools.partial(pick_kernel, period),
        out_shape=jax.ShapeDtypeStruct(options[0].shape, options[0].dtype),
        in_specs=[VMEM] * len(options),
        out_specs=VMEM,
        compiler_params=PARAMS,
    )(*options)


def halves(blocks, bit):
    keep = [block for block in blocks if not block >> bit & 1]
    return [block | 1 << bit for block in keep], keep


def product_kernel(orders, index, mine_ref, theirs_ref, here_ref, across_ref, *refs):
    outs, slab_ref = refs[:-1], refs[-1]
    row = lax.axis_index("row")
    holds = row // 2 + row % 2 == 1
    depth, width = here_ref.shape[1:]

    def build(piece_ref):
        real, imag = piece_ref[0], piece_ref[1]
        slab_ref[:depth, :width] = real
        slab_ref[:depth, width:] = imag
        slab_ref[depth:, :width] = -imag
        slab_ref[depth:, width:] = real

    pl.when(holds)(lambda: build(here_ref))
    pl.when(jnp.logical_not(holds))(lambda: build(across_ref))
    for order, left_ref, out_ref in zip(orders, (mine_ref, theirs_ref), outs):
        count, _, rows, _ = out_ref.shape
        blocks = halves(range(2 * count), order[0])[index]
        left = jnp.concatenate([left_ref[block * rows : (block + 1) * rows, :] for block in blocks])
        value = jnp.dot(left, slab_ref[...], preferred_element_type=jnp.float32).astype(out_ref.dtype)
        for place in range(count):
            for part in range(2):
                out_ref[place, part] = value[place * rows : (place + 1) * rows, part * width : (part + 1) * width]


def products(orders, index, mine, theirs, here, across, col_count):
    out = jax.ShapeDtypeStruct((col_count // 2, 2, mine.shape[0] // col_count, here.shape[2]), jnp.bfloat16)
    return pl.pallas_call(
        functools.partial(product_kernel, orders, index),
        out_shape=[out] * 2,
        in_specs=[VMEM] * 4,
        out_specs=[VMEM] * 2,
        scratch_shapes=[pltpu.VMEM((2 * here.shape[1], 2 * here.shape[2]), jnp.bfloat16)],
        compiler_params=PARAMS,
    )(mine, theirs, here, across)


def halve_kernel(orders, step, joined, *refs):
    ins, refs = refs[:4], refs[4:]
    outs = refs[-2:] if joined else refs[-4:]
    for chain, order in enumerate(orders):
        keep_ref, other_ref = ins[2 * chain : 2 * chain + 2]
        blocks = range(1 << len(order))
        for bit in order[:step]:
            blocks = halves(blocks, bit)[1]
        blocks = list(blocks)
        for index, kept in enumerate(halves(blocks, order[step])):
            for place, block in enumerate(kept):
                at = blocks.index(block)
                total = keep_ref[at].astype(jnp.float32) + other_ref[at].astype(jnp.float32)
                if joined:
                    outs[index][chain] = total.astype(outs[index].dtype)
                else:
                    out_ref = outs[2 * chain + index]
                    out_ref[out_ref.shape[0] - len(kept) + place] = total.astype(out_ref.dtype)
    if len(refs) > len(outs):
        outs[3][0] = refs[0][...]


def halve(orders, step, keeps, others, ready=None):
    blocks, *rest = keeps[0].shape
    last = step == len(orders[0]) - 1
    joined = last and orders[0][step] == orders[1][step]
    send = jax.ShapeDtypeStruct((2 if joined else blocks // 2, *rest), jnp.bfloat16)
    keep = jax.ShapeDtypeStruct(send.shape, jnp.float32)
    moving = jax.ShapeDtypeStruct((2, *rest), jnp.bfloat16)
    outs = pl.pallas_call(
        functools.partial(halve_kernel, orders, step, joined),
        out_shape=[send, keep] if joined else [send, keep, send, keep if ready is None else moving],
        in_specs=[VMEM] * (4 if ready is None else 5),
        out_specs=[VMEM] * (2 if joined else 4),
        compiler_params=PARAMS,
    )(keeps[0], others[0], keeps[1], others[1], *(() if ready is None else (ready,)))
    return outs[0::2], outs[1::2]


def add_kernel(joined, *refs):
    ins, outs = refs[:-2], refs[-2:]
    for chain, out_ref in enumerate(outs):
        keep_ref, other_ref = ins if joined else ins[2 * chain : 2 * chain + 2]
        at = chain if joined else 0
        out_ref[...] = (keep_ref[at] + other_ref[at].astype(jnp.float32)).astype(out_ref.dtype)


def add(keeps, others):
    return pl.pallas_call(
        functools.partial(add_kernel, len(keeps) == 1),
        out_shape=[jax.ShapeDtypeStruct(keeps[0].shape[1:], jnp.bfloat16)] * 2,
        in_specs=[VMEM] * (2 * len(keeps)),
        out_specs=[VMEM] * 2,
        compiler_params=PARAMS,
    )(*[value for pair in zip(keeps, others) for value in pair])


def finish_kernel(mine_ref, keep_ref, near_ref, moved_ref, far_ref, out_ref):
    core = lax.axis_index("row") % 2
    width = mine_ref.shape[-1]
    out_ref[core, :, :, :width] = mine_ref[...]
    out_ref[core, :, :, width:] = (keep_ref[0] + near_ref[0].astype(jnp.float32)).astype(out_ref.dtype)
    out_ref[1 - core, :, :, :width] = moved_ref[0]
    total = moved_ref[1].astype(jnp.float32) + far_ref[0].astype(jnp.float32)
    out_ref[1 - core, :, :, width:] = total.astype(out_ref.dtype)


def finish(mine, *parts):
    width = mine.shape[-1] + parts[0].shape[-1]
    return pl.pallas_call(
        finish_kernel,
        out_shape=jax.ShapeDtypeStruct((2, *mine.shape[:-1], width), jnp.bfloat16),
        in_specs=[VMEM] * (1 + len(parts)),
        out_specs=VMEM,
        compiler_params=PARAMS,
    )(mine, *parts)


def solution(mesh):
    row_count, col_count = mesh.shape["row"], mesh.shape["col"]
    x_count = col_count // row_count
    y_count = row_count // 2
    half_cols = col_count // 2
    every = range(row_count * col_count)
    x_bits = bits_of(x_count)
    z_bits = [bit for bit in bits_of(col_count) if bit not in x_bits]
    orders = (
        (x_bits + z_bits, z_bits[:1] + x_bits + z_bits[1:]),
        (x_bits + z_bits, z_bits[-1:] + x_bits + z_bits[:-1]),
    )
    steps = len(x_bits + z_bits)
    swap_core = [(r, r ^ 1) for r in range(row_count)]

    def exchange(value, bit):
        return lax.ppermute(value, "col", [(c, c ^ (1 << bit)) for c in range(col_count)])

    def filled(pairs):
        def apart(a, b):
            (row_a, col_a), (row_b, col_b) = divmod(a, col_count), divmod(b, col_count)
            far = abs(col_a // x_count - col_b // x_count) + abs(col_a % x_count - col_b % x_count)
            return 2 if a == b else 4 * far + 4 * abs(row_a // 2 - row_b // 2) + abs(row_a - row_b)

        senders = set(every) - {s for s, _ in pairs}
        receivers = set(every) - {t for _, t in pairs}
        while receivers:
            _, s, t = min((apart(s, t), s, t) for s in senders for t in receivers)
            senders.remove(s)
            receivers.remove(t)
            pairs = pairs + [(s, t)]
        return pairs

    def target(s, panel, h):
        return (2 - panel) * col_count + s * x_count + h

    def straight_pairs(h):
        return filled(
            [(s * col_count + p * half_cols, target(s, p, h)) for s in range(row_count) for p in range(2)]
        )

    def hop_pairs(h):
        return [(d, d ^ h if d % col_count % half_cols in (0, h) else d ^ col_count) for d in every]

    def spread_pairs():
        return filled(
            [
                (s * col_count + p * half_cols + h, target(s, p, h))
                for s in range(row_count)
                for p in range(2)
                for h in range(x_count)
            ]
        )

    def across_pairs():
        pairs = []
        for r in range(row_count):
            y, core = divmod(r, 2)
            pairs.append((r, r ^ 1 if y > 1 or y == core else r ^ 2))
        return pairs

    def to_all_y(here):
        across = lax.ppermute(here, "row", across_pairs())
        y = lax.axis_index("row") // 2
        if y_count > 2:
            slab = jnp.where(y + lax.axis_index("row") % 2 == 1, here, across)
            for bit in range(1, y_count.bit_length() - 1):
                got = lax.ppermute(slab, "row", [(r, r ^ (2 << bit)) for r in range(row_count)])
                slab = jnp.where((y >> bit) & 1 == 1, got, slab)
            return slab, slab
        return here, across

    def exchange_step(wave, sends, step):
        return [exchange(send, order[step]) for send, order in zip(sends, orders[wave])]

    def on_device(raw_blocks, occupancy, exponent):
        pieces, left = lay_out(raw_blocks, column_factors(occupancy, exponent), x_count)

        straight = [lax.ppermute(pieces[h], ("row", "col"), straight_pairs(h)) for h in range(x_count)]
        hopped = [pieces[x_count]]
        for h in range(1, x_count):
            hopped.append(lax.ppermute(pieces[x_count + h], ("row", "col"), hop_pairs(h)))
        second = pick(hopped, half_cols)
        first = pick([after(got, second) for got in straight], x_count)
        theirs = lax.ppermute(left, "row", swap_core)

        second = lax.ppermute(second, ("row", "col"), spread_pairs())
        slabs = [to_all_y(first), to_all_y(second)]

        sends = [[], []]
        sends[0] = products(orders[0], 0, left, theirs, *slabs[0], col_count)
        others = exchange_step(0, sends[0], 0)
        keeps = products(orders[0], 1, left, theirs, *[after(slab, sends[0][0]) for slab in slabs[0]], col_count)
        sends[1] = products(orders[1], 0, left, theirs, *[after(slab, keeps[0]) for slab in slabs[1]], col_count)
        later = exchange_step(1, sends[1], 0)
        others = [after(other, sends[1][0]) for other in others]
        sends[0], keeps = halve(orders[0], 1, keeps, others)
        others = exchange_step(0, sends[0], 1)
        stay = products(orders[1], 1, left, theirs, *[after(slab, sends[0][0]) for slab in slabs[1]], col_count)
        sends[0], keeps = halve(orders[0], 2, keeps, [after(other, stay[0]) for other in others])
        others = exchange_step(0, sends[0], 2)
        for step in range(1, steps):
            if step + 1 == steps - 1:
                mine, other_rows = add(keeps, others)
                mark = mine
            elif step + 1 < steps - 1:
                sends[0], keeps = halve(orders[0], step + 2, keeps, others)
                others = exchange_step(0, sends[0], step + 2)
                mark = sends[0][0]
            if step > 1:
                later = [after(other, mark) for other in later]
            sends[1], stay = halve(orders[1], step, stay, later, other_rows if step == steps - 1 else None)
            if step < steps - 1:
                later = exchange_step(1, sends[1], step)
        near = exchange(sends[1][0], orders[1][0][-1])
        across = [(d, d ^ col_count ^ (1 << orders[1][1][-1])) for d in every]
        far = lax.ppermute(sends[1][1], ("row", "col"), across)
        moved = lax.ppermute(stay[1], "row", swap_core)
        return finish(mine, stay[0], near, moved, far)

    placed = (P(None, "row", "col"), P("row", "col"), P("row", "col"))
    return jax.shard_map(
        on_device,
        mesh=mesh,
        in_specs=placed,
        out_specs=P(None, None, ("row", "col"), None),
        check_vma=False,
    )
```
